32 devices in a mesh: row: 4 (over y, x), col: 4 (over z), depth: 2 (over core).
Axes of the slice: x: 2, y: 2, z: 4, core: 2. Of those that a mesh axis runs over, the one named last changes fastest.
Arguments:
- features: bfloat16 [8192, 128], P(('row', 'col')), may hold values from -6 to 6
- self_weight: bfloat16 [128, 256], P(None, 'depth'), may hold values from -0.5 to 0.5
- neigh_weight: bfloat16 [128, 256], P(None, 'depth'), may hold values from -0.5 to 0.5
- bias: float32 [256], P('depth'), may hold values from -3 to 3
- cotangent: bfloat16 [8192, 256], P(('row', 'col'), 'depth'), may hold values from -6 to 6
- tile_values: bfloat16 [8192, 128, 128], P(('row', 'col', 'depth')), may hold values from -0.0625 to 0.0625
- tile_rows: int32 [32, 256], P(('row', 'col', 'depth')), may hold values from 0 to 15
- tile_cols: int32 [32, 256], P(('row', 'col', 'depth')), may hold values from 0 to 15
- tile_counts: int32 [32], P(('row', 'col', 'depth')), may hold values from 32 to 256, as said below
Outputs:
- output: bfloat16 [8192, 256], P(('row', 'col'), 'depth')
- grad_features: bfloat16 [8192, 128], P(('row', 'col', 'depth'))
- grad_self: float32 [128, 256], P(None, 'depth')
- grad_neigh: float32 [128, 256], P(None, 'depth')
- grad_bias: float32 [256], P('depth')
The draws below stay inside these ranges and needn't reach their ends.
Inputs may be any that keep to these rules, and one draw needn't show every extreme that they name: `tile_rows`: a row block below 16. `tile_cols`: a column block below 16. `tile_counts`: each device's count is 256 divided by 1, 2, 4 or 8; some device has all 256 slots live.
All inputs are finite; a program needn't handle non-finite values.
Results may differ from the reference program's by a relative error of at most 0.0057.
Values may be sent and summed in bfloat16 or wider, within the bound.
A program may use at most 64 MiB of HBM per device.

```python
import jax
import jax.numpy as jnp
from jax import lax

F = 128
H = 256
BLOCK = 128
SPAN = 512
TILES_DEV = 256
NODES = 8192
N_ROW = 4
N_COL = 4
N_DEPTH = 2


def draw_tile_counts(key, part):
    device_total = N_ROW * N_COL * N_DEPTH
    first_key, second_key = jax.random.split(jax.random.fold_in(key, 31))
    shifts = jax.random.randint(first_key, (device_total,), 0, 4, dtype=jnp.int32)
    counts = jnp.right_shift(jnp.full((device_total,), TILES_DEV, jnp.int32), shifts)
    busiest = jax.random.randint(second_key, (), 0, device_total, dtype=jnp.int32)
    counts = counts.at[busiest].set(TILES_DEV)
    return counts.astype(jnp.int32)


def place_ends(values, stream_key, low, high):
    shape = values.shape
    index_at = [jax.random.randint(jax.random.fold_in(stream_key, axis), (), 0, shape[axis]) for axis in range(len(shape))]
    values = values.at[tuple(index_at)].set(low)
    longest = shape.index(max(shape))
    index_at[longest] = (index_at[longest] + 1) % shape[longest]
    return values.at[tuple(index_at)].set(high)


def level_of(own_key, extent, shards, low, high):
    level = 1.0
    for position, parts in shards:
        heights = jax.random.uniform(jax.random.fold_in(jax.random.fold_in(own_key, 6), position), (parts,), jnp.float32, low / len(shards), high / len(shards))
        level = level * jnp.repeat(jnp.exp(heights), extent[position] // parts).reshape((-1,) + (1,) * (len(extent) - 1 - position))
    return level


def centred(stream_key, shape, scale, limit, shards=(), kind=jnp.bfloat16):
    loudness = level_of(stream_key, shape, shards, -0.22, 0.18) if shards else 1.0
    values = jax.random.normal(stream_key, shape, jnp.float32) * scale * loudness
    return jnp.minimum(jnp.maximum(values, -limit), limit).astype(kind)


def setup_inputs(seed: int = 0) -> dict:
    streams_of = jax.random.split(jax.random.key(seed), 10)
    return {
        "features": centred(streams_of[0], (NODES, F), 1.0, 6.0, ((0, 16),)),
        "self_weight": centred(streams_of[1], (F, H), F ** -0.5, 0.5, ((1, 2),)),
        "neigh_weight": centred(streams_of[2], (F, H), F ** -0.5, 0.5, ((1, 2),)),
        "bias": centred(streams_of[3], (H,), 0.5, 3.0, ((0, 2),), jnp.float32),
        "cotangent": centred(streams_of[4], (NODES, H), 1.0, 6.0, ((0, 16), (1, 2))),
        "tile_values": centred(streams_of[5], (N_ROW * N_COL * N_DEPTH * TILES_DEV, BLOCK, BLOCK), (TILES_DEV * BLOCK * BLOCK // SPAN) ** -0.5, 0.0625, ((0, 32),)),
        "tile_rows": place_ends(jax.random.randint(streams_of[6], (N_ROW * N_COL * N_DEPTH, TILES_DEV), 0, SPAN * N_COL // BLOCK), jax.random.fold_in(streams_of[6], 1), 0, (SPAN * N_COL // BLOCK) - 1).astype(jnp.int32),
        "tile_cols": place_ends(jax.random.randint(streams_of[7], (N_ROW * N_COL * N_DEPTH, TILES_DEV), 0, SPAN * N_ROW // BLOCK), jax.random.fold_in(streams_of[7], 1), 0, (SPAN * N_ROW // BLOCK) - 1).astype(jnp.int32),
        "tile_counts": draw_tile_counts(jax.random.fold_in(streams_of[9], 71), 0),
    }


def reference(features, self_weight, neigh_weight, bias, cotangent, tile_values, tile_rows, tile_cols, tile_counts):
    node_total = features.shape[0]
    hidden = self_weight.shape[1]
    blocks_span = SPAN // BLOCK
    block_total = node_total // BLOCK
    device_total = N_ROW * N_COL * N_DEPTH
    device_ids = jnp.arange(device_total, dtype=jnp.int32)
    group_row = device_ids // (N_COL * N_DEPTH)
    group_col = device_ids // N_DEPTH % N_COL
    out_block = (group_row[:, None] * (N_COL * blocks_span) + tile_rows).astype(jnp.int32)
    in_block = ((tile_cols // blocks_span * N_COL + group_col[:, None]) * blocks_span + tile_cols % blocks_span).astype(jnp.int32)
    live_mask = jnp.arange(TILES_DEV, dtype=jnp.int32)[None, :] < tile_counts[:, None]
    tile_stack = tile_values.reshape(device_total, TILES_DEV, BLOCK, BLOCK)
    transformed = jnp.dot(features, neigh_weight, preferred_element_type=jnp.float32).astype(jnp.bfloat16)
    source = transformed.reshape(block_total, BLOCK, hidden)

    def forward_step(totals, item):
        tile_block, out_index, in_index, alive = item
        product = jnp.einsum('tij,tjh->tih', tile_block.astype(jnp.float32), source[in_index].astype(jnp.float32))
        product = jnp.where(alive[:, None, None], product, 0.0)
        return (totals.at[out_index].add(product), None)
    aggregated, _ = lax.scan(forward_step, jnp.zeros((block_total, BLOCK, hidden), jnp.float32), (tile_stack, out_block, in_block, live_mask))
    preact = jnp.dot(features, self_weight, preferred_element_type=jnp.float32) + aggregated.reshape(node_total, hidden) + bias
    gate_value = jax.nn.sigmoid(preact)
    output = (preact * gate_value).astype(jnp.bfloat16)
    grad_pre = (cotangent.astype(jnp.float32) * gate_value * (1.0 + preact * (1.0 - gate_value))).astype(jnp.bfloat16)
    grad_source = grad_pre.reshape(block_total, BLOCK, hidden)

    def backward_step(totals, item):
        tile_block, out_index, in_index, alive = item
        product = jnp.einsum('tij,tih->tjh', tile_block.astype(jnp.float32), grad_source[out_index].astype(jnp.float32))
        product = jnp.where(alive[:, None, None], product, 0.0)
        return (totals.at[in_index].add(product), None)
    grad_sum, _ = lax.scan(backward_step, jnp.zeros((block_total, BLOCK, hidden), jnp.float32), (tile_stack, out_block, in_block, live_mask))
    grad_transformed = grad_sum.reshape(node_total, hidden).astype(jnp.bfloat16)
    grad_features = (jnp.dot(grad_pre, self_weight.T, preferred_element_type=jnp.float32) + jnp.dot(grad_transformed, neigh_weight.T, preferred_element_type=jnp.float32)).astype(jnp.bfloat16)
    grad_scale = 1.0 / jnp.sqrt(jnp.float32(node_total))
    grad_self = jnp.dot(features.T, grad_pre, preferred_element_type=jnp.float32) * grad_scale
    grad_neigh = jnp.dot(features.T, grad_transformed, preferred_element_type=jnp.float32) * grad_scale
    grad_bias = lax.optimization_barrier(jnp.sum(grad_pre.astype(jnp.float32), axis=0)) * grad_scale
    return (output, grad_features, grad_self, grad_neigh, grad_bias)
```

```python
import functools

import jax
import jax.numpy as jnp
from jax import lax
from jax.experimental import pallas as pl
from jax.experimental.pallas import tpu as pltpu
from jax.sharding import PartitionSpec as P

BF = jnp.bfloat16
F32 = jnp.float32


def dot(a, b, ca=1, cb=0):
    return lax.dot_general(a, b, (((ca,), (cb,)), ((), ())), preferred_element_type=F32)


def peer_order(n):
    return sorted(range(1, n), key=lambda k: (abs(2 * k - n), k))


def kernel(
    dims,
    feat,
    ws,
    wn,
    bias,
    cot,
    rows_ref,
    cols_ref,
    counts,
    tiles_hbm,
    out,
    gfeat,
    wout,
    tiles,
    run,
    dense,
    f_all,
    wsx,
    wnx,
    biasb,
    biasx,
    cotx,
    idx_v,
    idx_s,
    p_own,
    p_mate,
    p_x,
    s_b,
    z_x,
    o_mate,
    u_all,
    g_acc,
    g_own,
    g_mate,
    g_x,
    gs_b,
    gz_x,
    w_part,
    w_x,
    w_rx,
    w_2,
    w_cx,
    v_t,
    tile_sem,
    loc_sem,
    send_sem,
    recv_sem,
):
    nr, nc, n, block, slots, chunks = dims
    f = feat.shape[1]
    hh = ws.shape[1]
    half = n // 2
    rb = nc * n // block
    cb = nr * n // block
    r, c, d = lax.axis_index("row"), lax.axis_index("col"), lax.axis_index("depth")
    mate = (r, c, 1 - d)

    def row_peer(k):
        return lax.rem(r + k, nr)

    def col_peer(k):
        return lax.rem(c + k, nc)

    made = []

    def send(src, dst, device):
        i = len(made)
        copy = pltpu.make_async_remote_copy(
            src_ref=src,
            dst_ref=dst,
            send_sem=send_sem.at[i],
            recv_sem=recv_sem.at[i],
            device_id=device,
            device_id_type=pl.DeviceIdType.MESH,
        )
        copy.start()
        made.append(copy)
        return copy

    per = slots // chunks
    loads = []
    for i in range(chunks):
        part = pl.ds(i * per, per)
        load = pltpu.make_async_copy(tiles_hbm.at[part], tiles.at[part], tile_sem.at[i])
        load.start()
        loads.append(load)

    barrier = pltpu.get_barrier_semaphore()
    peers = [mate]
    peers += [(row_peer(k), c, d) for k in range(1, nr)]
    peers += [(r, col_peer(k), d) for k in range(1, nc)]
    for p in peers:
        pl.semaphore_signal(barrier, inc=1, device_id=p, device_id_type=pl.DeviceIdType.MESH)

    own_rows = pl.ds(pl.multiple_of(d * half, half), half)
    mate_rows = pl.ds(pl.multiple_of((1 - d) * half, half), half)
    live = counts[0]
    lane = lax.broadcasted_iota(jnp.int32, (slots, slots), 1)
    sub = lax.broadcasted_iota(jnp.int32, (slots, slots), 0)
    pos_row = jnp.broadcast_to(rows_ref[...] * cb + cols_ref[...], (slots, slots))
    pos_row = jnp.where(lane < live, pos_row, rb * cb)
    key_row = pos_row * slots + lane
    key_col = jnp.sum(jnp.where(lane == sub, key_row, 0), axis=1, keepdims=True)
    pos_col = jnp.sum(jnp.where(lane == sub, pos_row, 0), axis=1, keepdims=True)
    rank = jnp.sum((key_row < key_col).astype(jnp.int32), axis=1, keepdims=True)
    hit = rank == lane
    idx_v[0:1, 0:slots] = jnp.sum(jnp.where(hit, sub, 0), axis=0, keepdims=True)
    idx_v[1:2, 0:slots] = jnp.sum(jnp.where(hit, pos_col, 0), axis=0, keepdims=True)
    places = lax.broadcasted_iota(jnp.int32, (slots, rb * cb), 1)
    upto = jnp.sum((pos_col <= places).astype(jnp.int32), axis=0, keepdims=True)
    below = jnp.sum((pos_col < places).astype(jnp.int32), axis=0, keepdims=True)
    idx_v[2:3, 0 : rb * cb] = jnp.where(upto > below, upto - 1, slots)
    to_smem = pltpu.make_async_copy(idx_v, idx_s, loc_sem.at[0])
    to_smem.start()

    pl.semaphore_wait(barrier, len(peers))
    my_f = pl.ds(pl.multiple_of(r * n, n), n)
    biasb[...] = jnp.broadcast_to(bias[...], biasb.shape)
    feat_c = [send(feat, f_all.at[my_f], (row_peer(k), c, d)) for k in peer_order(nr)]
    early = [
        send(ws, wsx, mate),
        send(wn, wnx, mate),
        send(cot.at[mate_rows], cotx, mate),
        send(biasb, biasx, mate),
    ]
    f_all[my_f, :] = feat[...]
    run[slots] = jnp.zeros((block, block), BF)
    w_part[...] = jnp.zeros_like(w_part)
    to_smem.wait()
    for load in loads:
        load.wait()

    def merge(k, acc):
        same = idx_s[1, k] == idx_s[1, jnp.maximum(k - 1, 0)]
        acc = jnp.where(same, acc, 0.0) + tiles[idx_s[0, k]].astype(F32)
        run[k] = acc.astype(BF)
        return acc

    lax.fori_loop(0, slots, merge, jnp.zeros((block, block), F32), unroll=4)

    def place(i, carry):
        at = pl.ds(pl.multiple_of(i * block, block), block)
        for j in range(cb):
            dense[at, j * block : (j + 1) * block] = run[idx_s[2, i * cb + j]]
        return carry

    lax.fori_loop(0, rb, place, 0)

    for copy in feat_c:
        copy.wait_recv()

    def rows_at(owner, part):
        return pl.ds(pl.multiple_of(owner * n + part * half, half), half)

    x_c, z_c = {}, {}

    def finish(k):
        x_c[k].wait_recv()
        total = p_own[k] + p_x[k]
        if k == 0:
            p_own[0] = total
        else:
            s_b[k] = total.astype(BF)
            z_c[k] = send(s_b.at[k], z_x.at[k], (r, col_peer(k), d))

    order = peer_order(nc) + [0]
    for i, k in enumerate(order):
        owner = col_peer(k)
        p_mate[k] = dot(dense[rows_at(owner, 1 - d), :], f_all[...])
        x_c[k] = send(p_mate.at[k], p_x.at[k], mate)
        p_own[k] = dot(dense[rows_at(owner, d), :], f_all[...])
        if i:
            finish(order[i - 1])
    finish(order[-1])
    for copy in early:
        copy.wait_recv()
    f_own = feat[own_rows, :]
    agg = p_own[0]
    for k in peer_order(nc):
        z_c[k].wait_recv()
        agg = agg + z_x[k].astype(F32)

    hi = agg.astype(BF)
    lo = (agg - hi.astype(F32)).astype(BF)
    weights = [(ws[...], wn[...]), (wsx[...], wnx[...])]
    biases = [biasb[0:1, :], biasx[0:1, :]]
    cots = [cot[own_rows, :], cotx[...]]
    grads = []
    u_t = v = None
    for e in range(2):
        w_s, w_n = weights[e]
        pre = dot(f_own, w_s) + dot(hi, w_n) + dot(lo, w_n) + biases[e]
        gate = jax.nn.sigmoid(pre)
        value = (pre * gate).astype(BF)
        if e == 0:
            out[own_rows, :] = value
        else:
            o_mate[...] = value
        g = (cots[e].astype(F32) * gate * (1.0 + pre * (1.0 - gate))).astype(BF)
        grads.append(g)
        term = dot(w_n, g, 1, 1)
        u_t = term if u_t is None else u_t + term
    u_all[0, 0] = u_t.astype(BF)
    u_m = send(u_all.at[0, 0], u_all.at[0, 1], mate)
    u_c = {k: send(u_all.at[0, 0], u_all.at[k, 0], (r, col_peer(k), d)) for k in peer_order(nc)}
    out_c = send(o_mate, out.at[own_rows], mate)
    for e in (1, 0):
        g = grads[e]
        w_part[e, 0:f, :] = dot(f_own, g, 0, 0)
        w_part[e, f : 2 * f, :] = dot(hi, g, 0, 0)
        total = jnp.sum(g.astype(F32), axis=0, keepdims=True)
        w_part[e, 2 * f : 2 * f + 8, :] = jnp.broadcast_to(total, (8, hh))
        if e == 1:
            w_c = send(w_part.at[1], w_x, mate)
    v_t[...] = dot(weights[0][0], grads[0], 1, 1) + dot(weights[1][0], grads[1], 1, 1)

    def add_rows(k, e, first):
        owner = lax.rem(c - k + nc, nc)
        at = rows_at(owner, d if e == 0 else 1 - d)
        for q in range(nr):
            for h in range(2):
                col = q * n + h * half
                term = dot(u_all[k, e], dense[at, col : col + half])
                g_acc[q, h] = term if first else g_acc[q, h] + term

    add_rows(0, 0, True)

    w_rows = w_x.shape[0]
    wr = w_rows // nr
    wc = wr // nc
    w_c.wait_recv()
    w_part[0] = w_part[0] + w_x[...]
    wr_c = []
    for k in range(1, nr):
        at = pl.ds(pl.multiple_of(row_peer(k) * wr, 8), wr)
        wr_c.append(send(w_part.at[0, at], w_rx.at[k], (row_peer(k), c, d)))

    u_m.wait_recv()
    add_rows(0, 1, False)

    for copy in wr_c:
        copy.wait_recv()
    total = w_part[0, pl.ds(pl.multiple_of(r * wr, 8), wr), :]
    for k in range(1, nr):
        total = total + w_rx[k]
    w_2[...] = total
    wc_c = []
    for k in range(1, nc):
        at = pl.ds(pl.multiple_of(col_peer(k) * wc, 8), wc)
        wc_c.append(send(w_2.at[at], w_cx.at[k], (r, col_peer(k), d)))

    fwd_c = {}
    for k in reversed(peer_order(nc)):
        u_c[k].wait_recv()
        fwd_c[k] = send(u_all.at[k, 0], u_all.at[k, 1], mate)
        add_rows(k, 0, False)

    for copy in wc_c:
        copy.wait_recv()
    total = w_2[pl.ds(pl.multiple_of(c * wc, 8), wc), :]
    for k in range(1, nc):
        total = total + w_cx[k]
    mine = pl.ds(pl.multiple_of(r * wr + c * wc, 8), wc)
    wout[mine, :] = total * (1.0 / jnp.sqrt(jnp.full((1, 1), nr * nc * n, F32)))
    wg_c = [send(wout.at[mine], wout.at[mine], (r, col_peer(k), d)) for k in range(1, nc)]

    for copy in fwd_c.values():
        copy.wait_recv()

    def last_rows(owner, part):
        col = pl.ds(pl.multiple_of(owner * n + part * half, half), half)
        total = g_acc[owner, part]
        for k in peer_order(nc):
            at = rows_at(lax.rem(c - k + nc, nc), 1 - d)
            total = total + dot(u_all[k, 1], dense[at, col])
        return total

    gx_c, gz_c = {}, {}

    def finish_back(k):
        gx_c[k].wait_recv()
        total = g_own[k] + g_x[k]
        if k == 0:
            g_own[0] = total
        else:
            gs_b[k] = total.astype(BF)
            gz_c[k] = send(gs_b.at[k], gz_x.at[k], (row_peer(k), c, d))

    order = peer_order(nr) + [0]
    for i, k in enumerate(order):
        owner = row_peer(k)
        g_mate[k] = last_rows(owner, 1 - d)
        gx_c[k] = send(g_mate.at[k], g_x.at[k], mate)
        g_own[k] = last_rows(owner, d)
        if i:
            finish_back(order[i - 1])
    finish_back(order[-1])

    for copy in wg_c:
        copy.wait_recv()
    whole = pl.ds(pl.multiple_of(r * wr, 8), wr)
    ag_c = [send(wout.at[whole], wout.at[whole], (row_peer(k), c, d)) for k in range(1, nr)]

    total = v_t[...] + g_own[0]
    for k in peer_order(nr):
        gz_c[k].wait_recv()
        total = total + gz_x[k].astype(F32)
    gfeat[...] = total.T.astype(BF)

    out_c.wait_recv()
    for copy in ag_c:
        copy.wait_recv()
    for copy in made:
        copy.wait_send()


def body(mesh, features, self_weight, neigh_weight, bias, cotangent, tile_values, tile_rows, tile_cols, tile_counts):
    nr, nc, nd = mesh.shape["row"], mesh.shape["col"], mesh.shape["depth"]
    assert nd == 2
    n, f = features.shape
    hh = self_weight.shape[1]
    slots, block, _ = tile_values.shape
    half = n // nd
    rb, cb = nc * n // block, nr * n // block
    unit = nr * nc * 8
    w_rows = -(-(2 * f + 8) // unit) * unit
    chunks = 8
    width = max(slots, rb * cb)
    copies = 12 + 5 * nr + 6 * nc
    vmem = pl.BlockSpec(memory_space=pltpu.VMEM)
    dims = (nr, nc, n, block, slots, chunks)
    out, gfeat, wout = pl.pallas_call(
        functools.partial(kernel, dims),
        out_shape=(
            jax.ShapeDtypeStruct((n, hh), BF),
            jax.ShapeDtypeStruct((half, f), BF),
            jax.ShapeDtypeStruct((w_rows, hh), F32),
        ),
        in_specs=[vmem] * 7
        + [pl.BlockSpec(memory_space=pltpu.SMEM), pl.BlockSpec(memory_space=pl.ANY)],
        out_specs=(vmem, vmem, vmem),
        scratch_shapes=[
            pltpu.VMEM((slots, block, block), BF),
            pltpu.VMEM((slots + 1, block, block), BF),
            pltpu.VMEM((rb * block, cb * block), BF),
            pltpu.VMEM((nr * n, f), BF),
            pltpu.VMEM((f, hh), BF),
            pltpu.VMEM((f, hh), BF),
            pltpu.VMEM((8, hh), F32),
            pltpu.VMEM((8, hh), F32),
            pltpu.VMEM((half, hh), BF),
            pltpu.VMEM((8, width), jnp.int32),
            pltpu.SMEM((8, width), jnp.int32),
            pltpu.VMEM((nc, half, f), F32),
            pltpu.VMEM((nc, half, f), F32),
            pltpu.VMEM((nc, half, f), F32),
            pltpu.VMEM((nc, half, f), BF),
            pltpu.VMEM((nc, half, f), BF),
            pltpu.VMEM((half, hh), BF),
            pltpu.VMEM((nc, 2, f, half), BF),
            pltpu.VMEM((nr, 2, f, half), F32),
            pltpu.VMEM((nr, f, half), F32),
            pltpu.VMEM((nr, f, half), F32),
            pltpu.VMEM((nr, f, half), F32),
            pltpu.VMEM((nr, f, half), BF),
            pltpu.VMEM((nr, f, half), BF),
            pltpu.VMEM((2, w_rows, hh), F32),
            pltpu.VMEM((w_rows, hh), F32),
            pltpu.VMEM((nr, w_rows // nr, hh), F32),
            pltpu.VMEM((w_rows // nr, hh), F32),
            pltpu.VMEM((nc, w_rows // nr // nc, hh), F32),
            pltpu.VMEM((f, half), F32),
            pltpu.SemaphoreType.DMA((chunks,)),
            pltpu.SemaphoreType.DMA((1,)),
            pltpu.SemaphoreType.DMA((copies,)),
            pltpu.SemaphoreType.DMA((copies,)),
        ],
        compiler_params=pltpu.CompilerParams(
            collective_id=0, has_side_effects=True, vmem_limit_bytes=62 * 1024 * 1024
        ),
        name="sage_layer",
    )(
        features,
        self_weight,
        neigh_weight,
        bias.reshape(1, hh),
        cotangent,
        tile_rows,
        tile_cols,
        tile_counts,
        tile_values,
    )
    return out, gfeat, wout[:f], wout[f : 2 * f], wout[2 * f]


def solution(mesh):
    placed = (
        P(("row", "col"), None),
        P(None, "depth"),
        P(None, "depth"),
        P("depth"),
        P(("row", "col"), "depth"),
        P(("row", "col", "depth"), None, None),
        P(("row", "col", "depth"), None),
        P(("row", "col", "depth"), None),
        P(("row", "col", "depth")),
    )
    return jax.shard_map(
        functools.partial(body, mesh),
        mesh=mesh,
        in_specs=placed,
        out_specs=(
            P(("row", "col"), "depth"),
            P(("row", "col", "depth"), None),
            P(None, "depth"),
            P(None, "depth"),
            P("depth"),
        ),
        check_vma=False,
    )
```

```python
import functools

import jax
import jax.numpy as jnp
from jax import lax
from jax.experimental import pallas as pl
from jax.experimental.pallas import tpu as pltpu
from jax.sharding import PartitionSpec as P

BF = jnp.bfloat16
F32 = jnp.float32


def dot(a, b, ca=1, cb=0):
    return lax.dot_general(a, b, (((ca,), (cb,)), ((), ())), preferred_element_type=F32)


def peer_order(n):
    return sorted(range(1, n), key=lambda k: (abs(2 * k - n), k))


def kernel(
    dims,
    feat_hbm,
    ws_hbm,
    wn_hbm,
    bias,
    cot_hbm,
    rows_ref,
    cols_ref,
    counts,
    tiles_hbm,
    out,
    gfeat,
    wout,
    tiles,
    run,
    f_all,
    ws,
    wn,
    cot,
    wsx,
    wnx,
    biasb,
    biasx,
    cotx,
    idx_v,
    idx_s,
    p_own,
    p_mate,
    p_x,
    s_b,
    z_x,
    o_own,
    o_mate,
    u_all,
    g_acc,
    g_own,
    g_mate,
    g_x,
    gs_b,
    gz_x,
    w_part,
    w_x,
    w_rx,
    w_2,
    w_cx,
    v_t,
    pre_s,
    tile_sem,
    loc_sem,
    send_sem,
    recv_sem,
):
    nr, nc, n, block, slots, chunks = dims
    f = feat_hbm.shape[1]
    hh = ws.shape[1]
    half = n // 2
    rb = nc * n // block
    cb = nr * n // block
    r, c, d = lax.axis_index("row"), lax.axis_index("col"), lax.axis_index("depth")
    mate = (r, c, 1 - d)

    def row_peer(k):
        return lax.rem(r + k, nr)

    def col_peer(k):
        return lax.rem(c + k, nc)

    made = []

    def send(src, dst, device):
        i = len(made)
        copy = pltpu.make_async_remote_copy(
            src_ref=src,
            dst_ref=dst,
            send_sem=send_sem.at[i],
            recv_sem=recv_sem.at[i],
            device_id=device,
            device_id_type=pl.DeviceIdType.MESH,
        )
        copy.start()
        made.append(copy)
        return copy

    per = slots // chunks
    loads = []
    for i in range(chunks):
        part = pl.ds(i * per, per)
        load = pltpu.make_async_copy(tiles_hbm.at[part], tiles.at[part], tile_sem.at[i])
        load.start()
        loads.append(load)

    my_f = pl.ds(pl.multiple_of(r * n, n), n)
    own_rows = pl.ds(pl.multiple_of(d * half, half), half)
    mate_rows = pl.ds(pl.multiple_of((1 - d) * half, half), half)

    def f_rows(k):
        at = lax.rem(r - k + nr, nr) * n + d * half
        return pl.ds(pl.multiple_of(at, half), half)

    def bring(i, src, dst):
        load = pltpu.make_async_copy(src, dst, loc_sem.at[i])
        load.start()
        return load

    brought = [
        bring(0, feat_hbm, f_all.at[my_f]),
        bring(1, ws_hbm, ws),
        bring(2, wn_hbm, wn),
        bring(3, cot_hbm.at[own_rows], cot),
    ]

    barrier = pltpu.get_barrier_semaphore()
    peers = [mate]
    peers += [(row_peer(k), c, d) for k in range(1, nr)]
    peers += [(r, col_peer(k), d) for k in range(1, nc)]
    for p in peers:
        pl.semaphore_signal(barrier, inc=1, device_id=p, device_id_type=pl.DeviceIdType.MESH)

    live = counts[0]
    lane = lax.broadcasted_iota(jnp.int32, (slots, slots), 1)
    sub = lax.broadcasted_iota(jnp.int32, (slots, slots), 0)
    pos_row = jnp.broadcast_to(rows_ref[...] * cb + cols_ref[...], (slots, slots))
    pos_row = jnp.where(lane < live, pos_row, rb * cb)
    key_row = pos_row * slots + lane
    key_col = jnp.sum(jnp.where(lane == sub, key_row, 0), axis=1, keepdims=True)
    pos_col = jnp.sum(jnp.where(lane == sub, pos_row, 0), axis=1, keepdims=True)
    rank = jnp.sum((key_row < key_col).astype(jnp.int32), axis=1, keepdims=True)
    hit = rank == lane
    idx_v[0:1, 0:slots] = jnp.sum(jnp.where(hit, sub, 0), axis=0, keepdims=True)
    idx_v[1:2, 0:slots] = jnp.sum(jnp.where(hit, pos_col, 0), axis=0, keepdims=True)
    places = lax.broadcasted_iota(jnp.int32, (slots, rb * cb), 1)
    upto = jnp.sum((pos_col <= places).astype(jnp.int32), axis=0, keepdims=True)
    below = jnp.sum((pos_col < places).astype(jnp.int32), axis=0, keepdims=True)
    idx_v[2:3, 0 : rb * cb] = jnp.where(upto > below, upto - 1, slots)
    to_smem = pltpu.make_async_copy(idx_v, idx_s, loc_sem.at[4])
    to_smem.start()

    pl.semaphore_wait(barrier, len(peers))
    biasb[...] = jnp.broadcast_to(bias[...], biasb.shape)
    feat_c = {
        k: send(feat_hbm.at[own_rows], f_all.at[f_rows(0)], (row_peer(k), c, d))
        for k in peer_order(nr)
    }
    early = [
        send(ws_hbm, wsx, mate),
        send(wn_hbm, wnx, mate),
        send(cot_hbm.at[mate_rows], cotx, mate),
        send(biasb, biasx, mate),
    ]
    run[slots] = jnp.zeros((block, block), BF)
    w_part[...] = jnp.zeros_like(w_part)
    to_smem.wait()
    for load in loads:
        load.wait()

    def merge(k, acc):
        same = idx_s[1, k] == idx_s[1, jnp.maximum(k - 1, 0)]
        acc = jnp.where(same, acc, 0.0) + tiles[idx_s[0, k]].astype(F32)
        run[k] = acc.astype(BF)
        return acc

    acc = jnp.zeros((block, block), F32)
    acc = lax.fori_loop(0, slots // 2, merge, acc, unroll=8)
    pair_c = []
    for k in peer_order(nr):
        feat_c[k].wait_recv()
        pair_c.append(send(f_all.at[f_rows(k)], f_all.at[f_rows(k)], mate))
    lax.fori_loop(slots // 2, slots, merge, acc, unroll=8)

    def merged(first_row, first_col, height, width):
        lines = []
        for i in range(height):
            at = (first_row + i) * cb + first_col
            line = [run[idx_s[2, at + j]] for j in range(width)]
            lines.append(jnp.concatenate(line, axis=1))
        return jnp.concatenate(lines, axis=0)

    for load in brought:
        load.wait()
    for copy in pair_c:
        copy.wait_recv()

    hb = half // block

    def rows_at(owner, part):
        return (owner * 2 + part) * hb

    def product(owner, part):
        return dot(merged(rows_at(owner, part), 0, hb, cb), f_all[...])

    x_c, z_c = {}, {}

    def finish(k):
        x_c[k].wait_recv()
        total = p_own[k] + p_x[k]
        if k == 0:
            p_own[0] = total
        else:
            s_b[k] = total.astype(BF)
            z_c[k] = send(s_b.at[k], z_x.at[k], (r, col_peer(k), d))

    order = peer_order(nc) + [0]
    for i, k in enumerate(order):
        owner = col_peer(k)
        p_mate[k] = product(owner, 1 - d)
        x_c[k] = send(p_mate.at[k], p_x.at[k], mate)
        p_own[k] = product(owner, d)
        if i:
            finish(order[i - 1])
    finish(order[-1])
    for copy in early:
        copy.wait_recv()
    f_own = f_all[f_rows(0), :]
    weights = [(ws[...], wn[...]), (wsx[...], wnx[...])]
    biases = [biasb[0:1, :], biasx[0:1, :]]
    for e in range(2):
        pre_s[e] = dot(f_own, weights[e][0]) + biases[e]
    agg = p_own[0]
    for k in peer_order(nc):
        z_c[k].wait_recv()
        agg = agg + z_x[k].astype(F32)

    hi = agg.astype(BF)
    lo = (agg - hi.astype(F32)).astype(BF)
    cots = [cot[...], cotx[...]]
    grads = []
    u_t = v = None
    for e in range(2):
        w_n = weights[e][1]
        pre = pre_s[e] + dot(hi, w_n) + dot(lo, w_n)
        gate = jax.nn.sigmoid(pre)
        value = (pre * gate).astype(BF)
        if e == 0:
            o_own[...] = value
        else:
            o_mate[...] = value
        g = (cots[e].astype(F32) * gate * (1.0 + pre * (1.0 - gate))).astype(BF)
        grads.append(g)
        term = dot(w_n, g, 1, 1)
        u_t = term if u_t is None else u_t + term
    u_all[0, 0] = u_t.astype(BF)
    u_m = send(u_all.at[0, 0], u_all.at[0, 1], mate)
    u_c = {k: send(u_all.at[0, 0], u_all.at[k, 0], (r, col_peer(k), d)) for k in peer_order(nc)}
    out_c = send(o_mate, out.at[own_rows], mate)
    kept = bring(0, o_own, out.at[own_rows])
    for e in (1, 0):
        g = grads[e]
        w_part[e, 0:f, :] = dot(f_own, g, 0, 0)
        w_part[e, f : 2 * f, :] = dot(hi, g, 0, 0)
        total = jnp.sum(g.astype(F32), axis=0, keepdims=True)
        w_part[e, 2 * f : 2 * f + 8, :] = jnp.broadcast_to(total, (8, hh))
        if e == 1:
            w_c = send(w_part.at[1], w_x, mate)
    v_t[...] = dot(weights[0][0], grads[0], 1, 1) + dot(weights[1][0], grads[1], 1, 1)

    def add_rows(k, e, first):
        owner = lax.rem(c - k + nc, nc)
        at = rows_at(owner, d if e == 0 else 1 - d)
        for q in range(nr):
            for h in range(2):
                term = dot(u_all[k, e], merged(at, (q * 2 + h) * hb, hb, hb))
                g_acc[q, h] = term if first else g_acc[q, h] + term

    add_rows(0, 0, True)

    w_rows = w_x.shape[0]
    wr = w_rows // nr
    wc = wr // nc
    w_c.wait_recv()
    w_part[0] = w_part[0] + w_x[...]
    wr_c = []
    for k in range(1, nr):
        at = pl.ds(pl.multiple_of(row_peer(k) * wr, 8), wr)
        wr_c.append(send(w_part.at[0, at], w_rx.at[k], (row_peer(k), c, d)))

    u_m.wait_recv()
    add_rows(0, 1, False)

    for copy in wr_c:
        copy.wait_recv()
    total = w_part[0, pl.ds(pl.multiple_of(r * wr, 8), wr), :]
    for k in range(1, nr):
        total = total + w_rx[k]
    w_2[...] = total
    wc_c = []
    for k in range(1, nc):
        at = pl.ds(pl.multiple_of(col_peer(k) * wc, 8), wc)
        wc_c.append(send(w_2.at[at], w_cx.at[k], (r, col_peer(k), d)))

    arrivals = list(reversed(peer_order(nc)))
    fwd_c = {}
    for i, k in enumerate(arrivals):
        u_c[k].wait_recv()
        fwd_c[k] = send(u_all.at[k, 0], u_all.at[k, 1], mate)
        if i:
            fwd_c[arrivals[i - 1]].wait_recv()
            add_rows(arrivals[i - 1], 1, False)
        add_rows(k, 0, False)

    for copy in wc_c:
        copy.wait_recv()
    total = w_2[pl.ds(pl.multiple_of(c * wc, 8), wc), :]
    for k in range(1, nc):
        total = total + w_cx[k]
    mine = pl.ds(pl.multiple_of(r * wr + c * wc, 8), wc)
    wout[mine, :] = total * (1.0 / jnp.sqrt(jnp.full((1, 1), nr * nc * n, F32)))
    wg_c = [send(wout.at[mine], wout.at[mine], (r, col_peer(k), d)) for k in range(1, nc)]

    last = arrivals[-1]
    fwd_c[last].wait_recv()

    def last_rows(owner, part):
        at = rows_at(lax.rem(c - last + nc, nc), 1 - d)
        blocks = merged(at, (owner * 2 + part) * hb, hb, hb)
        return g_acc[owner, part] + dot(u_all[last, 1], blocks)

    gx_c, gz_c = {}, {}

    def finish_back(k):
        gx_c[k].wait_recv()
        total = g_own[k] + g_x[k]
        if k == 0:
            g_own[0] = total
        else:
            gs_b[k] = total.astype(BF)
            gz_c[k] = send(gs_b.at[k], gz_x.at[k], (row_peer(k), c, d))

    order = peer_order(nr) + [0]
    for i, k in enumerate(order):
        owner = row_peer(k)
        g_mate[k] = last_rows(owner, 1 - d)
        gx_c[k] = send(g_mate.at[k], g_x.at[k], mate)
        g_own[k] = last_rows(owner, d)
        if i:
            finish_back(order[i - 1])
    finish_back(order[-1])

    for copy in wg_c:
        copy.wait_recv()
    whole = pl.ds(pl.multiple_of(r * wr, 8), wr)
    ag_c = [send(wout.at[whole], wout.at[whole], (row_peer(k), c, d)) for k in range(1, nr)]

    total = v_t[...] + g_own[0]
    for k in peer_order(nr):
        gz_c[k].wait_recv()
        total = total + gz_x[k].astype(F32)
    gfeat[...] = total.T.astype(BF)

    kept.wait()
    out_c.wait_recv()
    for copy in ag_c:
        copy.wait_recv()
    for copy in made:
        copy.wait_send()


def hand_out(out, gfeat, wout, out_o, gfeat_o, self_o, neigh_o, bias_o, sem):
    f = self_o.shape[0]
    pairs = [
        (out, out_o),
        (gfeat, gfeat_o),
        (wout.at[pl.ds(0, f)], self_o),
        (wout.at[pl.ds(f, f)], neigh_o),
        (wout.at[pl.ds(2 * f, 1)], bias_o),
    ]
    copies = [pltpu.make_async_copy(a, b, sem.at[i]) for i, (a, b) in enumerate(pairs)]
    for copy in copies:
        copy.start()
    for copy in copies:
        copy.wait()


def body(mesh, features, self_weight, neigh_weight, bias, cotangent, tile_values, tile_rows, tile_cols, tile_counts):
    nr, nc, nd = mesh.shape["row"], mesh.shape["col"], mesh.shape["depth"]
    assert nd == 2
    n, f = features.shape
    hh = self_weight.shape[1]
    slots, block, _ = tile_values.shape
    half = n // nd
    rb, cb = nc * n // block, nr * n // block
    unit = nr * nc * 8
    w_rows = -(-(2 * f + 8) // unit) * unit
    chunks = 8
    width = max(slots, rb * cb)
    copies = 12 + 6 * nr + 6 * nc
    vmem = pl.BlockSpec(memory_space=pltpu.VMEM)
    smem = pl.BlockSpec(memory_space=pltpu.SMEM)
    hbm = pl.BlockSpec(memory_space=pl.ANY)
    dims = (nr, nc, n, block, slots, chunks)
    out, gfeat, wout = pl.pallas_call(
        functools.partial(kernel, dims),
        out_shape=(
            jax.ShapeDtypeStruct((n, hh), BF),
            jax.ShapeDtypeStruct((half, f), BF),
            jax.ShapeDtypeStruct((w_rows, hh), F32),
        ),
        in_specs=[hbm, hbm, hbm, vmem, hbm, vmem, vmem, smem, hbm],
        out_specs=(hbm, vmem, vmem),
        scratch_shapes=[
            pltpu.VMEM((slots, block, block), BF),
            pltpu.VMEM((slots + 1, block, block), BF),
            pltpu.VMEM((nr * n, f), BF),
            pltpu.VMEM((f, hh), BF),
            pltpu.VMEM((f, hh), BF),
            pltpu.VMEM((half, hh), BF),
            pltpu.VMEM((f, hh), BF),
            pltpu.VMEM((f, hh), BF),
            pltpu.VMEM((8, hh), F32),
            pltpu.VMEM((8, hh), F32),
            pltpu.VMEM((half, hh), BF),
            pltpu.VMEM((8, width), jnp.int32),
            pltpu.SMEM((8, width), jnp.int32),
            pltpu.VMEM((nc, half, f), F32),
            pltpu.VMEM((nc, half, f), F32),
            pltpu.VMEM((nc, half, f), F32),
            pltpu.VMEM((nc, half, f), BF),
            pltpu.VMEM((nc, half, f), BF),
            pltpu.VMEM((half, hh), BF),
            pltpu.VMEM((half, hh), BF),
            pltpu.VMEM((nc, 2, f, half), BF),
            pltpu.VMEM((nr, 2, f, half), F32),
            pltpu.VMEM((nr, f, half), F32),
            pltpu.VMEM((nr, f, half), F32),
            pltpu.VMEM((nr, f, half), F32),
            pltpu.VMEM((nr, f, half), BF),
            pltpu.VMEM((nr, f, half), BF),
            pltpu.VMEM((2, w_rows, hh), F32),
            pltpu.VMEM((w_rows, hh), F32),
            pltpu.VMEM((nr, w_rows // nr, hh), F32),
            pltpu.VMEM((w_rows // nr, hh), F32),
            pltpu.VMEM((nc, w_rows // nr // nc, hh), F32),
            pltpu.VMEM((f, half), F32),
            pltpu.VMEM((2, half, hh), F32),
            pltpu.SemaphoreType.DMA((chunks,)),
            pltpu.SemaphoreType.DMA((5,)),
            pltpu.SemaphoreType.DMA((copies,)),
            pltpu.SemaphoreType.DMA((copies,)),
        ],
        compiler_params=pltpu.CompilerParams(
            collective_id=0, has_side_effects=True, vmem_limit_bytes=60 * 1024 * 1024
        ),
        name="sage_layer",
    )(
        features,
        self_weight,
        neigh_weight,
        bias.reshape(1, hh),
        cotangent,
        tile_rows,
        tile_cols,
        tile_counts,
        tile_values,
    )
    out, gfeat, g_self, g_neigh, g_bias = pl.pallas_call(
        hand_out,
        out_shape=(
            jax.ShapeDtypeStruct((n, hh), BF),
            jax.ShapeDtypeStruct((half, f), BF),
            jax.ShapeDtypeStruct((f, hh), F32),
            jax.ShapeDtypeStruct((f, hh), F32),
            jax.ShapeDtypeStruct((1, hh), F32),
        ),
        in_specs=[hbm] * 3,
        out_specs=(hbm,) * 5,
        scratch_shapes=[pltpu.SemaphoreType.DMA((5,))],
        name="hand_out",
    )(out, gfeat, wout)
    return out, gfeat, g_self, g_neigh, g_bias.reshape(hh)


def solution(mesh):
    placed = (
        P(("row", "col"), None),
        P(None, "depth"),
        P(None, "depth"),
        P("depth"),
        P(("row", "col"), "depth"),
        P(("row", "col", "depth"), None, None),
        P(("row", "col", "depth"), None),
        P(("row", "col", "depth"), None),
        P(("row", "col", "depth")),
    )
    return jax.shard_map(
        functools.partial(body, mesh),
        mesh=mesh,
        in_specs=placed,
        out_specs=(
            P(("row", "col"), "depth"),
            P(("row", "col", "depth"), None),
            P(None, "depth"),
            P(None, "depth"),
            P("depth"),
        ),
        check_vma=False,
    )
```

```python
import functools

import jax
import jax.numpy as jnp
from jax import lax
from jax.experimental import pallas as pl
from jax.experimental.pallas import tpu as pltpu
from jax.sharding import PartitionSpec as P

BF = jnp.bfloat16
F32 = jnp.float32


def dot(a, b, ca=1, cb=0):
    return lax.dot_general(a, b, (((ca,), (cb,)), ((), ())), preferred_element_type=F32)


def peer_order(n):
    return sorted(range(1, n), key=lambda k: (abs(2 * k - n), k))


def kernel(
    dims,
    feat_hbm,
    ws_hbm,
    wn_hbm,
    bias,
    cot_hbm,
    rows_ref,
    cols_ref,
    counts,
    tiles_hbm,
    out,
    gfeat,
    wout,
    tiles,
    run,
    f_all,
    ws,
    wn,
    cot,
    wsx,
    wnx,
    biasb,
    biasx,
    cotx,
    idx_v,
    idx_s,
    p_own,
    p_mate,
    p_x,
    s_b,
    z_x,
    o_own,
    o_mate,
    u_all,
    g_acc,
    g_own,
    g_mate,
    g_x,
    gs_b,
    gz_x,
    w_part,
    w_x,
    w_rx,
    w_2,
    w_cx,
    v_t,
    pre_s,
    hi_s,
    g_s,
    tile_sem,
    loc_sem,
    send_sem,
    recv_sem,
):
    nr, nc, n, block, slots, chunks = dims
    f = feat_hbm.shape[1]
    hh = ws.shape[1]
    half = n // 2
    rb = nc * n // block
    cb = nr * n // block
    r, c, d = lax.axis_index("row"), lax.axis_index("col"), lax.axis_index("depth")
    mate = (r, c, 1 - d)

    def row_peer(k):
        return lax.rem(r + k, nr)

    def col_peer(k):
        return lax.rem(c + k, nc)

    made = []

    def send(src, dst, device):
        i = len(made)
        copy = pltpu.make_async_remote_copy(
            src_ref=src,
            dst_ref=dst,
            send_sem=send_sem.at[i],
            recv_sem=recv_sem.at[i],
            device_id=device,
            device_id_type=pl.DeviceIdType.MESH,
        )
        copy.start()
        made.append(copy)
        return copy

    per = slots // chunks
    loads = []
    for i in range(chunks):
        part = pl.ds(i * per, per)
        load = pltpu.make_async_copy(tiles_hbm.at[part], tiles.at[part], tile_sem.at[i])
        load.start()
        loads.append(load)

    my_f = pl.ds(pl.multiple_of(r * n, n), n)
    own_rows = pl.ds(pl.multiple_of(d * half, half), half)
    mate_rows = pl.ds(pl.multiple_of((1 - d) * half, half), half)

    def f_rows(k):
        at = lax.rem(r - k + nr, nr) * n + d * half
        return pl.ds(pl.multiple_of(at, half), half)

    def bring(i, src, dst):
        load = pltpu.make_async_copy(src, dst, loc_sem.at[i])
        load.start()
        return load

    brought = [
        bring(0, feat_hbm, f_all.at[my_f]),
        bring(1, ws_hbm, ws),
        bring(2, wn_hbm, wn),
        bring(3, cot_hbm, cot),
    ]

    barrier = pltpu.get_barrier_semaphore()
    peers = [mate]
    peers += [(row_peer(k), c, d) for k in range(1, nr)]
    peers += [(r, col_peer(k), d) for k in range(1, nc)]
    for p in peers:
        pl.semaphore_signal(barrier, inc=1, device_id=p, device_id_type=pl.DeviceIdType.MESH)

    live = counts[0]
    lane = lax.broadcasted_iota(jnp.int32, (slots, slots), 1)
    sub = lax.broadcasted_iota(jnp.int32, (slots, slots), 0)
    pos_row = jnp.broadcast_to(rows_ref[...] * cb + cols_ref[...], (slots, slots))
    pos_row = jnp.where(lane < live, pos_row, rb * cb)
    key_row = pos_row * slots + lane
    key_col = jnp.sum(jnp.where(lane == sub, key_row, 0), axis=1, keepdims=True)
    pos_col = jnp.sum(jnp.where(lane == sub, pos_row, 0), axis=1, keepdims=True)
    rank = jnp.sum((key_row < key_col).astype(jnp.int32), axis=1, keepdims=True)
    hit = rank == lane
    idx_v[0:1, 0:slots] = jnp.sum(jnp.where(hit, sub, 0), axis=0, keepdims=True)
    idx_v[1:2, 0:slots] = jnp.sum(jnp.where(hit, pos_col, 0), axis=0, keepdims=True)
    places = lax.broadcasted_iota(jnp.int32, (slots, rb * cb), 1)
    upto = jnp.sum((pos_col <= places).astype(jnp.int32), axis=0, keepdims=True)
    below = jnp.sum((pos_col < places).astype(jnp.int32), axis=0, keepdims=True)
    idx_v[2:3, 0 : rb * cb] = jnp.where(upto > below, upto - 1, slots)
    to_smem = pltpu.make_async_copy(idx_v, idx_s, loc_sem.at[4])
    to_smem.start()

    for load in brought:
        load.wait()
    pl.semaphore_wait(barrier, len(peers))
    biasb[...] = jnp.broadcast_to(bias[...], biasb.shape)
    feat_c = {
        k: send(f_all.at[f_rows(0)], f_all.at[f_rows(0)], (row_peer(k), c, d))
        for k in peer_order(nr)
    }
    early = [
        send(ws, wsx, mate),
        send(wn, wnx, mate),
        send(cot.at[mate_rows], cotx, mate),
        send(biasb, biasx, mate),
    ]
    run[slots] = jnp.zeros((block, block), BF)
    w_part[...] = jnp.zeros_like(w_part)
    to_smem.wait()
    for load in loads:
        load.wait()

    def merge(k, acc):
        same = idx_s[1, k] == idx_s[1, jnp.maximum(k - 1, 0)]
        acc = jnp.where(same, acc, 0.0) + tiles[idx_s[0, k]].astype(F32)
        run[k] = acc.astype(BF)
        return acc

    acc = jnp.zeros((block, block), F32)
    acc = lax.fori_loop(0, slots // 2, merge, acc, unroll=8)
    pair_c = []
    for k in peer_order(nr):
        feat_c[k].wait_recv()
        pair_c.append(send(f_all.at[f_rows(k)], f_all.at[f_rows(k)], mate))
    lax.fori_loop(slots // 2, slots, merge, acc, unroll=8)

    def merged(lines_at, first_col, width):
        lines = []
        for at in lines_at:
            line = [run[idx_s[2, at * cb + first_col + j]] for j in range(width)]
            lines.append(jnp.concatenate(line, axis=1))
        return jnp.concatenate(lines, axis=0)

    for copy in pair_c:
        copy.wait_recv()

    part = half // 2
    pb = part // block

    def lines(owner, core, s):
        return [((owner * 2 + core) * 2 + s) * pb + i for i in range(pb)]

    x_c, z_c = {}, {}

    def finish(s, k):
        x_c[s, k].wait_recv()
        total = p_own[s, k] + p_x[s, k]
        if k == 0:
            p_own[s, 0] = total
        else:
            s_b[s, k] = total.astype(BF)
            z_c[s, k] = send(s_b.at[s, k], z_x.at[s, k], (r, col_peer(k), d))

    steps = [(s, k) for s in range(2) for k in peer_order(nc) + [0]]
    for i, (s, k) in enumerate(steps):
        owner = col_peer(k)
        both = dot(merged(lines(owner, 1 - d, s) + lines(owner, d, s), 0, cb), f_all[...])
        p_mate[s, k] = both[:part]
        x_c[s, k] = send(p_mate.at[s, k], p_x.at[s, k], mate)
        p_own[s, k] = both[part:]
        if i:
            finish(*steps[i - 1])
    finish(*steps[-1])
    for copy in early:
        copy.wait_recv()
    f_own = f_all[f_rows(0), :]
    weights = [(ws[...], wn[...]), (wsx[...], wnx[...])]
    biases = [biasb[0:1, :], biasx[0:1, :]]
    for e in range(2):
        pre_s[e] = dot(f_own, weights[e][0]) + biases[e]

    u_m, u_c = [], {}
    for s in range(2):
        at = slice(s * part, (s + 1) * part)
        agg = p_own[s, 0]
        for k in peer_order(nc):
            z_c[s, k].wait_recv()
            agg = agg + z_x[s, k].astype(F32)
        hi = agg.astype(BF)
        lo = (agg - hi.astype(F32)).astype(BF)
        hi_s[at, :] = hi
        u_t = None
        for e in range(2):
            w_n = weights[e][1]
            pre = pre_s[e, at, :] + dot(hi, w_n) + dot(lo, w_n)
            gate = jax.nn.sigmoid(pre)
            value = (pre * gate).astype(BF)
            if e == 0:
                o_own[at, :] = value
                ct = cot[pl.ds(pl.multiple_of(d * half + s * part, part), part), :]
            else:
                o_mate[at, :] = value
                ct = cotx[at, :]
            g = (ct.astype(F32) * gate * (1.0 + pre * (1.0 - gate))).astype(BF)
            g_s[e, at, :] = g
            term = dot(w_n, g, 1, 1)
            u_t = term if u_t is None else u_t + term
        u_all[s, 0, 0] = u_t.astype(BF)
        for k in peer_order(nc):
            u_c[s, k] = send(u_all.at[s, 0, 0], u_all.at[s, k, 0], (r, col_peer(k), d))
        u_m.append(send(u_all.at[s, 0, 0], u_all.at[s, 0, 1], mate))
    out_c = send(o_mate, out.at[own_rows], mate)
    kept = bring(0, o_own, out.at[own_rows])
    hi = hi_s[...]
    grads = [g_s[0], g_s[1]]
    for e in (1, 0):
        g = grads[e]
        w_part[e, 0:f, :] = dot(f_own, g, 0, 0)
        w_part[e, f : 2 * f, :] = dot(hi, g, 0, 0)
        total = jnp.sum(g.astype(F32), axis=0, keepdims=True)
        w_part[e, 2 * f : 2 * f + 8, :] = jnp.broadcast_to(total, (8, hh))
        if e == 1:
            w_c = send(w_part.at[1], w_x, mate)
    v_t[...] = dot(weights[0][0], grads[0], 1, 1) + dot(weights[1][0], grads[1], 1, 1)

    def rows_term(s, k, first_col):
        owner = lax.rem(c - k + nc, nc)
        left = jnp.concatenate([u_all[s, k, 0], u_all[s, k, 1]], axis=1)
        return dot(left, merged(lines(owner, d, s) + lines(owner, 1 - d, s), first_col, 2 * pb))

    def add_rows(s, k, first=False):
        for q in range(nr):
            for h in range(2):
                term = rows_term(s, k, (q * 2 + h) * 2 * pb)
                g_acc[q, h] = term if first else g_acc[q, h] + term

    u_m[0].wait_recv()
    add_rows(0, 0, True)

    w_rows = w_x.shape[0]
    wr = w_rows // nr
    wc = wr // nc
    w_c.wait_recv()
    w_part[0] = w_part[0] + w_x[...]
    wr_c = []
    for k in range(1, nr):
        at = pl.ds(pl.multiple_of(row_peer(k) * wr, 8), wr)
        wr_c.append(send(w_part.at[0, at], w_rx.at[k], (row_peer(k), c, d)))

    u_m[1].wait_recv()
    add_rows(1, 0)

    for copy in wr_c:
        copy.wait_recv()
    total = w_part[0, pl.ds(pl.multiple_of(r * wr, 8), wr), :]
    for k in range(1, nr):
        total = total + w_rx[k]
    w_2[...] = total
    wc_c = []
    for k in range(1, nc):
        at = pl.ds(pl.multiple_of(col_peer(k) * wc, 8), wc)
        wc_c.append(send(w_2.at[at], w_cx.at[k], (r, col_peer(k), d)))

    arrivals = [(s, k) for s in range(2) for k in peer_order(nc)]
    fwd_c = {}
    for i, (s, k) in enumerate(arrivals):
        u_c[s, k].wait_recv()
        fwd_c[s, k] = send(u_all.at[s, k, 0], u_all.at[s, k, 1], mate)
        if i:
            fwd_c[arrivals[i - 1]].wait_recv()
            add_rows(*arrivals[i - 1])

    for copy in wc_c:
        copy.wait_recv()
    total = w_2[pl.ds(pl.multiple_of(c * wc, 8), wc), :]
    for k in range(1, nc):
        total = total + w_cx[k]
    mine = pl.ds(pl.multiple_of(r * wr + c * wc, 8), wc)
    wout[mine, :] = total * (1.0 / jnp.sqrt(jnp.full((1, 1), nr * nc * n, F32)))
    wg_c = [send(wout.at[mine], wout.at[mine], (r, col_peer(k), d)) for k in range(1, nc)]

    last = arrivals[-1]
    fwd_c[last].wait_recv()

    def last_rows(owner, core):
        return g_acc[owner, core] + rows_term(*last, (owner * 2 + core) * 2 * pb)

    gx_c, gz_c = {}, {}

    def finish_back(k):
        gx_c[k].wait_recv()
        total = g_own[k] + g_x[k]
        if k == 0:
            g_own[0] = total
        else:
            gs_b[k] = total.astype(BF)
            gz_c[k] = send(gs_b.at[k], gz_x.at[k], (row_peer(k), c, d))

    order = peer_order(nr) + [0]
    for i, k in enumerate(order):
        owner = row_peer(k)
        g_mate[k] = last_rows(owner, 1 - d)
        gx_c[k] = send(g_mate.at[k], g_x.at[k], mate)
        g_own[k] = last_rows(owner, d)
        if i:
            finish_back(order[i - 1])
    finish_back(order[-1])

    for copy in wg_c:
        copy.wait_recv()
    whole = pl.ds(pl.multiple_of(r * wr, 8), wr)
    ag_c = [send(wout.at[whole], wout.at[whole], (row_peer(k), c, d)) for k in range(1, nr)]

    total = v_t[...] + g_own[0]
    for k in peer_order(nr):
        gz_c[k].wait_recv()
        total = total + gz_x[k].astype(F32)
    gfeat[...] = total.T.astype(BF)

    kept.wait()
    out_c.wait_recv()
    for copy in ag_c:
        copy.wait_recv()
    for copy in made:
        copy.wait_send()


def hand_out(out, gfeat, wout, out_o, gfeat_o, self_o, neigh_o, bias_o):
    f = self_o.shape[0]
    out_o[...] = out[...]
    gfeat_o[...] = gfeat[...]
    self_o[...] = wout[0:f, :]
    neigh_o[...] = wout[f : 2 * f, :]
    bias_o[...] = wout[2 * f : 2 * f + 1, :]


def body(mesh, features, self_weight, neigh_weight, bias, cotangent, tile_values, tile_rows, tile_cols, tile_counts):
    nr, nc, nd = mesh.shape["row"], mesh.shape["col"], mesh.shape["depth"]
    assert nd == 2
    n, f = features.shape
    hh = self_weight.shape[1]
    slots, block, _ = tile_values.shape
    half = n // nd
    rb, cb = nc * n // block, nr * n // block
    unit = nr * nc * 8
    w_rows = -(-(2 * f + 8) // unit) * unit
    chunks = 8
    width = max(slots, rb * cb)
    copies = 12 + 6 * nr + 9 * nc
    vmem = pl.BlockSpec(memory_space=pltpu.VMEM)
    smem = pl.BlockSpec(memory_space=pltpu.SMEM)
    hbm = pl.BlockSpec(memory_space=pl.ANY)
    dims = (nr, nc, n, block, slots, chunks)
    out, gfeat, wout = pl.pallas_call(
        functools.partial(kernel, dims),
        out_shape=(
            jax.ShapeDtypeStruct((n, hh), BF),
            jax.ShapeDtypeStruct((half, f), BF),
            jax.ShapeDtypeStruct((w_rows, hh), F32),
        ),
        in_specs=[hbm, hbm, hbm, vmem, hbm, vmem, vmem, smem, hbm],
        out_specs=(hbm, vmem, vmem),
        scratch_shapes=[
            pltpu.VMEM((slots, block, block), BF),
            pltpu.VMEM((slots + 1, block, block), BF),
            pltpu.VMEM((nr * n, f), BF),
            pltpu.VMEM((f, hh), BF),
            pltpu.VMEM((f, hh), BF),
            pltpu.VMEM((n, hh), BF),
            pltpu.VMEM((f, hh), BF),
            pltpu.VMEM((f, hh), BF),
            pltpu.VMEM((8, hh), F32),
            pltpu.VMEM((8, hh), F32),
            pltpu.VMEM((half, hh), BF),
            pltpu.VMEM((8, width), jnp.int32),
            pltpu.SMEM((8, width), jnp.int32),
            pltpu.VMEM((2, nc, half // 2, f), F32),
            pltpu.VMEM((2, nc, half // 2, f), F32),
            pltpu.VMEM((2, nc, half // 2, f), F32),
            pltpu.VMEM((2, nc, half // 2, f), BF),
            pltpu.VMEM((2, nc, half // 2, f), BF),
            pltpu.VMEM((half, hh), BF),
            pltpu.VMEM((half, hh), BF),
            pltpu.VMEM((2, nc, 2, f, half // 2), BF),
            pltpu.VMEM((nr, 2, f, half), F32),
            pltpu.VMEM((nr, f, half), F32),
            pltpu.VMEM((nr, f, half), F32),
            pltpu.VMEM((nr, f, half), F32),
            pltpu.VMEM((nr, f, half), BF),
            pltpu.VMEM((nr, f, half), BF),
            pltpu.VMEM((2, w_rows, hh), F32),
            pltpu.VMEM((w_rows, hh), F32),
            pltpu.VMEM((nr, w_rows // nr, hh), F32),
            pltpu.VMEM((w_rows // nr, hh), F32),
            pltpu.VMEM((nc, w_rows // nr // nc, hh), F32),
            pltpu.VMEM((f, half), F32),
            pltpu.VMEM((2, half, hh), F32),
            pltpu.VMEM((half, f), BF),
            pltpu.VMEM((2, half, hh), BF),
            pltpu.SemaphoreType.DMA((chunks,)),
            pltpu.SemaphoreType.DMA((5,)),
            pltpu.SemaphoreType.DMA((copies,)),
            pltpu.SemaphoreType.DMA((copies,)),
        ],
        compiler_params=pltpu.CompilerParams(
            collective_id=0, has_side_effects=True, vmem_limit_bytes=60 * 1024 * 1024
        ),
        name="sage_layer",
    )(
        features,
        self_weight,
        neigh_weight,
        bias.reshape(1, hh),
        cotangent,
        tile_rows,
        tile_cols,
        tile_counts,
        tile_values,
    )
    out, gfeat, g_self, g_neigh, g_bias = pl.pallas_call(
        hand_out,
        out_shape=(
            jax.ShapeDtypeStruct((n, hh), BF),
            jax.ShapeDtypeStruct((half, f), BF),
            jax.ShapeDtypeStruct((f, hh), F32),
            jax.ShapeDtypeStruct((f, hh), F32),
            jax.ShapeDtypeStruct((1, hh), F32),
        ),
        in_specs=[vmem] * 3,
        out_specs=(vmem,) * 5,
        name="hand_out",
    )(out, gfeat, wout)
    return out, gfeat, g_self, g_neigh, g_bias.reshape(hh)


def solution(mesh):
    placed = (
        P(("row", "col"), None),
        P(None, "depth"),
        P(None, "depth"),
        P("depth"),
        P(("row", "col"), "depth"),
        P(("row", "col", "depth"), None, None),
        P(("row", "col", "depth"), None),
        P(("row", "col", "depth"), None),
        P(("row", "col", "depth")),
    )
    return jax.shard_map(
        functools.partial(body, mesh),
        mesh=mesh,
        in_specs=placed,
        out_specs=(
            P(("row", "col"), "depth"),
            P(("row", "col", "depth"), None),
            P(None, "depth"),
            P(None, "depth"),
            P("depth"),
        ),
        check_vma=False,
    )
```

```python
import functools

import jax
import jax.numpy as jnp
from jax import lax
from jax.experimental import pallas as pl
from jax.experimental.pallas import tpu as pltpu
from jax.sharding import PartitionSpec as P

BF = jnp.bfloat16
F32 = jnp.float32


def dot(a, b, ca=1, cb=0):
    return lax.dot_general(a, b, (((ca,), (cb,)), ((), ())), preferred_element_type=F32)


def peer_order(n):
    return sorted(range(1, n), key=lambda k: (abs(2 * k - n), k))


def kernel(
    dims,
    feat_hbm,
    ws_hbm,
    wn_hbm,
    bias,
    cot_hbm,
    rows_ref,
    cols_ref,
    counts,
    tiles_hbm,
    out,
    gfeat,
    wout,
    tiles,
    run,
    f_all,
    ws,
    wn,
    cot,
    wsx,
    wnx,
    biasb,
    biasx,
    cotx,
    idx_v,
    idx_s,
    p_own,
    p_mate,
    p_x,
    s_b,
    z_x,
    o_own,
    o_mate,
    u_all,
    g_acc,
    g_own,
    g_mate,
    g_x,
    gs_b,
    gz_x,
    w_part,
    w_x,
    w_rx,
    w_2,
    w_cx,
    v_t,
    pre_s,
    hi_s,
    g_s,
    tile_sem,
    loc_sem,
    send_sem,
    recv_sem,
):
    nr, nc, n, block, slots, chunks = dims
    f = feat_hbm.shape[1]
    hh = ws.shape[1]
    half = n // 2
    rb = nc * n // block
    cb = nr * n // block
    r, c, d = lax.axis_index("row"), lax.axis_index("col"), lax.axis_index("depth")
    mate = (r, c, 1 - d)

    def row_peer(k):
        return lax.rem(r + k, nr)

    def col_peer(k):
        return lax.rem(c + k, nc)

    made = []

    def send(src, dst, device):
        i = len(made)
        copy = pltpu.make_async_remote_copy(
            src_ref=src,
            dst_ref=dst,
            send_sem=send_sem.at[i],
            recv_sem=recv_sem.at[i],
            device_id=device,
            device_id_type=pl.DeviceIdType.MESH,
        )
        copy.start()
        made.append(copy)
        return copy

    my_f = pl.ds(pl.multiple_of(r * n, n), n)
    own_rows = pl.ds(pl.multiple_of(d * half, half), half)
    mate_rows = pl.ds(pl.multiple_of((1 - d) * half, half), half)

    def f_rows(k):
        at = lax.rem(r - k + nr, nr) * n + d * half
        return pl.ds(pl.multiple_of(at, half), half)

    def bring(i, src, dst):
        load = pltpu.make_async_copy(src, dst, loc_sem.at[i])
        load.start()
        return load

    brought = [
        bring(0, feat_hbm, f_all.at[my_f]),
        bring(1, ws_hbm, ws),
        bring(2, wn_hbm, wn),
        bring(3, cot_hbm, cot),
    ]

    per = slots // chunks
    loads = []
    for i in range(chunks):
        part = pl.ds(i * per, per)
        load = pltpu.make_async_copy(tiles_hbm.at[part], tiles.at[part], tile_sem.at[i])
        load.start()
        loads.append(load)

    barrier = pltpu.get_barrier_semaphore()
    peers = [mate]
    peers += [(row_peer(k), c, d) for k in range(1, nr)]
    peers += [(r, col_peer(k), d) for k in range(1, nc)]
    for p in peers:
        pl.semaphore_signal(barrier, inc=1, device_id=p, device_id_type=pl.DeviceIdType.MESH)

    live = counts[0]
    lane = lax.broadcasted_iota(jnp.int32, (slots, slots), 1)
    sub = lax.broadcasted_iota(jnp.int32, (slots, slots), 0)
    pos_row = jnp.broadcast_to(rows_ref[...] * cb + cols_ref[...], (slots, slots))
    pos_row = jnp.where(lane < live, pos_row, rb * cb)
    key_row = pos_row * slots + lane
    key_col = jnp.sum(jnp.where(lane == sub, key_row, 0), axis=1, keepdims=True)
    pos_col = jnp.sum(jnp.where(lane == sub, pos_row, 0), axis=1, keepdims=True)
    rank = jnp.sum((key_row < key_col).astype(jnp.int32), axis=1, keepdims=True)
    hit = rank == lane
    idx_v[0:1, 0:slots] = jnp.sum(jnp.where(hit, sub, 0), axis=0, keepdims=True)
    idx_v[1:2, 0:slots] = jnp.sum(jnp.where(hit, pos_col, 0), axis=0, keepdims=True)
    places = lax.broadcasted_iota(jnp.int32, (slots, rb * cb), 1)
    upto = jnp.sum((pos_col <= places).astype(jnp.int32), axis=0, keepdims=True)
    below = jnp.sum((pos_col < places).astype(jnp.int32), axis=0, keepdims=True)
    idx_v[2:3, 0 : rb * cb] = jnp.where(upto > below, upto - 1, slots)
    to_smem = pltpu.make_async_copy(idx_v, idx_s, loc_sem.at[4])
    to_smem.start()

    for load in brought:
        load.wait()
    pl.semaphore_wait(barrier, len(peers))
    biasb[...] = jnp.broadcast_to(bias[...], biasb.shape)
    feat_c = {
        k: send(f_all.at[f_rows(0)], f_all.at[f_rows(0)], (row_peer(k), c, d))
        for k in peer_order(nr)
    }
    early = [
        send(ws, wsx, mate),
        send(wn, wnx, mate),
        send(cot.at[mate_rows], cotx, mate),
        send(biasb, biasx, mate),
    ]
    run[slots] = jnp.zeros((block, block), BF)
    w_part[...] = jnp.zeros_like(w_part)
    to_smem.wait()
    for load in loads:
        load.wait()

    def merge(k, acc):
        same = idx_s[1, k] == idx_s[1, jnp.maximum(k - 1, 0)]
        acc = jnp.where(same, acc, 0.0) + tiles[idx_s[0, k]].astype(F32)
        run[k] = acc.astype(BF)
        return acc

    acc = jnp.zeros((block, block), F32)
    acc = lax.fori_loop(0, slots // 2, merge, acc, unroll=8)
    pair_c = []
    for k in peer_order(nr):
        feat_c[k].wait_recv()
        pair_c.append(send(f_all.at[f_rows(k)], f_all.at[f_rows(k)], mate))
    lax.fori_loop(slots // 2, slots, merge, acc, unroll=8)

    def merged(lines_at, first_col, width):
        lines = []
        for at in lines_at:
            line = [run[idx_s[2, at * cb + first_col + j]] for j in range(width)]
            lines.append(jnp.concatenate(line, axis=1))
        return jnp.concatenate(lines, axis=0)

    for copy in pair_c:
        copy.wait_recv()

    part = half // 2
    pb = part // block

    def lines(owner, core, s):
        return [((owner * 2 + core) * 2 + s) * pb + i for i in range(pb)]

    x_c, z_c = {}, {}

    def finish(s, k):
        x_c[s, k].wait_recv()
        total = p_own[s, k] + p_x[s, k]
        if k == 0:
            p_own[s, 0] = total
        else:
            s_b[s, k] = total.astype(BF)
            z_c[s, k] = send(s_b.at[s, k], z_x.at[s, k], (r, col_peer(k), d))

    steps = [(s, k) for s in range(2) for k in peer_order(nc) + [0]]
    for i, (s, k) in enumerate(steps):
        owner = col_peer(k)
        both = dot(merged(lines(owner, 1 - d, s) + lines(owner, d, s), 0, cb), f_all[...])
        p_mate[s, k] = both[:part]
        x_c[s, k] = send(p_mate.at[s, k], p_x.at[s, k], mate)
        p_own[s, k] = both[part:]
        if i:
            finish(*steps[i - 1])
    finish(*steps[-1])
    for copy in early:
        copy.wait_recv()
    f_own = f_all[f_rows(0), :]
    weights = [(ws[...], wn[...]), (wsx[...], wnx[...])]
    biases = [biasb[0:1, :], biasx[0:1, :]]
    for e in range(2):
        pre_s[e] = dot(f_own, weights[e][0]) + biases[e]

    u_m, u_c = [], {}
    for s in range(2):
        at = slice(s * part, (s + 1) * part)
        agg = p_own[s, 0]
        for k in peer_order(nc):
            z_c[s, k].wait_recv()
            agg = agg + z_x[s, k].astype(F32)
        hi = agg.astype(BF)
        lo = (agg - hi.astype(F32)).astype(BF)
        hi_s[at, :] = hi
        u_t = None
        for e in range(2):
            w_n = weights[e][1]
            pre = pre_s[e, at, :] + dot(hi, w_n) + dot(lo, w_n)
            gate = jax.nn.sigmoid(pre)
            value = (pre * gate).astype(BF)
            if e == 0:
                o_own[at, :] = value
                ct = cot[pl.ds(pl.multiple_of(d * half + s * part, part), part), :]
            else:
                o_mate[at, :] = value
                ct = cotx[at, :]
            g = (ct.astype(F32) * gate * (1.0 + pre * (1.0 - gate))).astype(BF)
            g_s[e, at, :] = g
            term = dot(w_n, g, 1, 1)
            u_t = term if u_t is None else u_t + term
        u_all[s, 0, 0] = u_t.astype(BF)
        for k in peer_order(nc):
            u_c[s, k] = send(u_all.at[s, 0, 0], u_all.at[s, k, 0], (r, col_peer(k), d))
        u_m.append(send(u_all.at[s, 0, 0], u_all.at[s, 0, 1], mate))
    out_c = send(o_mate, out.at[own_rows], mate)
    kept = bring(0, o_own, out.at[own_rows])
    hi = hi_s[...]
    grads = [g_s[0], g_s[1]]
    for e in (1, 0):
        g = grads[e]
        w_part[e, 0:f, :] = dot(f_own, g, 0, 0)
        w_part[e, f : 2 * f, :] = dot(hi, g, 0, 0)
        total = jnp.sum(g.astype(F32), axis=0, keepdims=True)
        w_part[e, 2 * f : 2 * f + 8, :] = jnp.broadcast_to(total, (8, hh))
        if e == 1:
            w_c = send(w_part.at[1], w_x, mate)
    v_t[...] = dot(weights[0][0], grads[0], 1, 1) + dot(weights[1][0], grads[1], 1, 1)

    def rows_term(s, k, first_col):
        owner = lax.rem(c - k + nc, nc)
        left = jnp.concatenate([u_all[s, k, 0], u_all[s, k, 1]], axis=1)
        return dot(left, merged(lines(owner, d, s) + lines(owner, 1 - d, s), first_col, 2 * pb))

    def add_rows(s, k, first=False):
        for q in range(nr):
            for h in range(2):
                term = rows_term(s, k, (q * 2 + h) * 2 * pb)
                g_acc[q, h] = term if first else g_acc[q, h] + term

    u_m[0].wait_recv()
    add_rows(0, 0, True)

    w_rows = w_x.shape[0]
    wr = w_rows // nr
    wc = wr // nc
    w_c.wait_recv()
    w_part[0] = w_part[0] + w_x[...]
    wr_c = []
    for k in range(1, nr):
        at = pl.ds(pl.multiple_of(row_peer(k) * wr, 8), wr)
        wr_c.append(send(w_part.at[0, at], w_rx.at[k], (row_peer(k), c, d)))

    u_m[1].wait_recv()
    add_rows(1, 0)

    for copy in wr_c:
        copy.wait_recv()
    total = w_part[0, pl.ds(pl.multiple_of(r * wr, 8), wr), :]
    for k in range(1, nr):
        total = total + w_rx[k]
    w_2[...] = total
    wc_c = []
    for k in range(1, nc):
        at = pl.ds(pl.multiple_of(col_peer(k) * wc, 8), wc)
        wc_c.append(send(w_2.at[at], w_cx.at[k], (r, col_peer(k), d)))

    arrivals = [(s, k) for s in range(2) for k in peer_order(nc)]
    fwd_c = {}
    for i, (s, k) in enumerate(arrivals):
        u_c[s, k].wait_recv()
        fwd_c[s, k] = send(u_all.at[s, k, 0], u_all.at[s, k, 1], mate)
        if i:
            fwd_c[arrivals[i - 1]].wait_recv()
            add_rows(*arrivals[i - 1])
        if i == 1:
            for copy in wc_c:
                copy.wait_recv()
            total = w_2[pl.ds(pl.multiple_of(c * wc, 8), wc), :]
            for k in range(1, nc):
                total = total + w_cx[k]
            mine = pl.ds(pl.multiple_of(r * wr + c * wc, 8), wc)
            wout[mine, :] = total * (1.0 / jnp.sqrt(jnp.full((1, 1), nr * nc * n, F32)))
            wg_c = [send(wout.at[mine], wout.at[mine], (r, col_peer(k), d)) for k in range(1, nc)]
        if i == len(arrivals) - 2:
            for copy in wg_c:
                copy.wait_recv()
            whole = pl.ds(pl.multiple_of(r * wr, 8), wr)
            ag_c = [send(wout.at[whole], wout.at[whole], (row_peer(k), c, d)) for k in range(1, nr)]

    last = arrivals[-1]
    fwd_c[last].wait_recv()

    def last_rows(owner, core):
        return g_acc[owner, core] + rows_term(*last, (owner * 2 + core) * 2 * pb)

    gx_c, gz_c = {}, {}

    def finish_back(k):
        gx_c[k].wait_recv()
        total = g_own[k] + g_x[k]
        if k == 0:
            g_own[0] = total
        else:
            gs_b[k] = total.astype(BF)
            gz_c[k] = send(gs_b.at[k], gz_x.at[k], (row_peer(k), c, d))

    order = peer_order(nr) + [0]
    for i, k in enumerate(order):
        owner = row_peer(k)
        g_mate[k] = last_rows(owner, 1 - d)
        gx_c[k] = send(g_mate.at[k], g_x.at[k], mate)
        g_own[k] = last_rows(owner, d)
        if i:
            finish_back(order[i - 1])
    finish_back(order[-1])

    total = v_t[...] + g_own[0]
    for k in peer_order(nr):
        gz_c[k].wait_recv()
        total = total + gz_x[k].astype(F32)
    gfeat[...] = total.T.astype(BF)

    kept.wait()
    out_c.wait_recv()
    for copy in ag_c:
        copy.wait_recv()
    for copy in made:
        copy.wait_send()


def hand_out(out, gfeat, wout, out_o, gfeat_o, self_o, neigh_o, bias_o):
    f = self_o.shape[0]
    out_o[...] = out[...]
    gfeat_o[...] = gfeat[...]
    self_o[...] = wout[0:f, :]
    neigh_o[...] = wout[f : 2 * f, :]
    bias_o[...] = wout[2 * f : 2 * f + 1, :]


def body(mesh, features, self_weight, neigh_weight, bias, cotangent, tile_values, tile_rows, tile_cols, tile_counts):
    nr, nc, nd = mesh.shape["row"], mesh.shape["col"], mesh.shape["depth"]
    assert nd == 2
    n, f = features.shape
    hh = self_weight.shape[1]
    slots, block, _ = tile_values.shape
    half = n // nd
    rb, cb = nc * n // block, nr * n // block
    unit = nr * nc * 8
    w_rows = -(-(2 * f + 8) // unit) * unit
    chunks = 8
    width = max(slots, rb * cb)
    copies = 12 + 6 * nr + 9 * nc
    vmem = pl.BlockSpec(memory_space=pltpu.VMEM)
    smem = pl.BlockSpec(memory_space=pltpu.SMEM)
    hbm = pl.BlockSpec(memory_space=pl.ANY)
    dims = (nr, nc, n, block, slots, chunks)
    out, gfeat, wout = pl.pallas_call(
        functools.partial(kernel, dims),
        out_shape=(
            jax.ShapeDtypeStruct((n, hh), BF),
            jax.ShapeDtypeStruct((half, f), BF),
            jax.ShapeDtypeStruct((w_rows, hh), F32),
        ),
        in_specs=[hbm, hbm, hbm, vmem, hbm, vmem, vmem, smem, hbm],
        out_specs=(hbm, vmem, vmem),
        scratch_shapes=[
            pltpu.VMEM((slots, block, block), BF),
            pltpu.VMEM((slots + 1, block, block), BF),
            pltpu.VMEM((nr * n, f), BF),
            pltpu.VMEM((f, hh), BF),
            pltpu.VMEM((f, hh), BF),
            pltpu.VMEM((n, hh), BF),
            pltpu.VMEM((f, hh), BF),
            pltpu.VMEM((f, hh), BF),
            pltpu.VMEM((8, hh), F32),
            pltpu.VMEM((8, hh), F32),
            pltpu.VMEM((half, hh), BF),
            pltpu.VMEM((8, width), jnp.int32),
            pltpu.SMEM((8, width), jnp.int32),
            pltpu.VMEM((2, nc, half // 2, f), F32),
            pltpu.VMEM((2, nc, half // 2, f), F32),
            pltpu.VMEM((2, nc, half // 2, f), F32),
            pltpu.VMEM((2, nc, half // 2, f), BF),
            pltpu.VMEM((2, nc, half // 2, f), BF),
            pltpu.VMEM((half, hh), BF),
            pltpu.VMEM((half, hh), BF),
            pltpu.VMEM((2, nc, 2, f, half // 2), BF),
            pltpu.VMEM((nr, 2, f, half), F32),
            pltpu.VMEM((nr, f, half), F32),
            pltpu.VMEM((nr, f, half), F32),
            pltpu.VMEM((nr, f, half), F32),
            pltpu.VMEM((nr, f, half), BF),
            pltpu.VMEM((nr, f, half), BF),
            pltpu.VMEM((2, w_rows, hh), F32),
            pltpu.VMEM((w_rows, hh), F32),
            pltpu.VMEM((nr, w_rows // nr, hh), F32),
            pltpu.VMEM((w_rows // nr, hh), F32),
            pltpu.VMEM((nc, w_rows // nr // nc, hh), F32),
            pltpu.VMEM((f, half), F32),
            pltpu.VMEM((2, half, hh), F32),
            pltpu.VMEM((half, f), BF),
            pltpu.VMEM((2, half, hh), BF),
            pltpu.SemaphoreType.DMA((chunks,)),
            pltpu.SemaphoreType.DMA((5,)),
            pltpu.SemaphoreType.DMA((copies,)),
            pltpu.SemaphoreType.DMA((copies,)),
        ],
        compiler_params=pltpu.CompilerParams(
            collective_id=0, has_side_effects=True, vmem_limit_bytes=60 * 1024 * 1024
        ),
        name="sage_layer",
    )(
        features,
        self_weight,
        neigh_weight,
        bias.reshape(1, hh),
        cotangent,
        tile_rows,
        tile_cols,
        tile_counts,
        tile_values,
    )
    out, gfeat, g_self, g_neigh, g_bias = pl.pallas_call(
        hand_out,
        out_shape=(
            jax.ShapeDtypeStruct((n, hh), BF),
            jax.ShapeDtypeStruct((half, f), BF),
            jax.ShapeDtypeStruct((f, hh), F32),
            jax.ShapeDtypeStruct((f, hh), F32),
            jax.ShapeDtypeStruct((1, hh), F32),
        ),
        in_specs=[vmem] * 3,
        out_specs=(vmem,) * 5,
        name="hand_out",
    )(out, gfeat, wout)
    return out, gfeat, g_self, g_neigh, g_bias.reshape(hh)


def solution(mesh):
    placed = (
        P(("row", "col"), None),
        P(None, "depth"),
        P(None, "depth"),
        P("depth"),
        P(("row", "col"), "depth"),
        P(("row", "col", "depth"), None, None),
        P(("row", "col", "depth"), None),
        P(("row", "col", "depth"), None),
        P(("row", "col", "depth")),
    )
    return jax.shard_map(
        functools.partial(body, mesh),
        mesh=mesh,
        in_specs=placed,
        out_specs=(
            P(("row", "col"), "depth"),
            P(("row", "col", "depth"), None),
            P(None, "depth"),
            P(None, "depth"),
            P("depth"),
        ),
        check_vma=False,
    )
```

```python
import functools

import jax
import jax.numpy as jnp
from jax import lax
from jax.experimental import pallas as pl
from jax.experimental.pallas import tpu as pltpu
from jax.sharding import PartitionSpec as P

BF = jnp.bfloat16
F32 = jnp.float32


def dot(a, b, ca=1, cb=0):
    return lax.dot_general(a, b, (((ca,), (cb,)), ((), ())), preferred_element_type=F32)


def peer_order(n):
    return sorted(range(1, n), key=lambda k: (abs(2 * k - n), k))


def kernel(
    dims,
    feat_hbm,
    ws_hbm,
    wn_hbm,
    bias,
    cot_hbm,
    rows_ref,
    cols_ref,
    counts,
    tiles_hbm,
    out,
    gfeat,
    wout,
    tiles,
    run,
    f_all,
    ws,
    wn,
    cot,
    wsx,
    wnx,
    biasb,
    biasx,
    cotx,
    idx_v,
    idx_s,
    p_own,
    p_mate,
    p_x,
    s_b,
    z_x,
    o_own,
    o_mate,
    u_all,
    g_acc,
    g_own,
    g_mate,
    g_x,
    gs_b,
    gz_x,
    w_part,
    w_x,
    w_rx,
    w_2,
    w_cx,
    v_t,
    pre_s,
    tile_sem,
    loc_sem,
    send_sem,
    recv_sem,
):
    nr, nc, n, block, slots, chunks = dims
    f = feat_hbm.shape[1]
    hh = ws.shape[1]
    half = n // 2
    rb = nc * n // block
    cb = nr * n // block
    r, c, d = lax.axis_index("row"), lax.axis_index("col"), lax.axis_index("depth")
    mate = (r, c, 1 - d)

    def row_peer(k):
        return lax.rem(r + k, nr)

    def col_peer(k):
        return lax.rem(c + k, nc)

    made = []

    def send(src, dst, device):
        i = len(made)
        copy = pltpu.make_async_remote_copy(
            src_ref=src,
            dst_ref=dst,
            send_sem=send_sem.at[i],
            recv_sem=recv_sem.at[i],
            device_id=device,
            device_id_type=pl.DeviceIdType.MESH,
        )
        copy.start()
        made.append(copy)
        return copy

    per = slots // chunks
    loads = []
    for i in range(chunks):
        part = pl.ds(i * per, per)
        load = pltpu.make_async_copy(tiles_hbm.at[part], tiles.at[part], tile_sem.at[i])
        load.start()
        loads.append(load)

    my_f = pl.ds(pl.multiple_of(r * n, n), n)
    own_rows = pl.ds(pl.multiple_of(d * half, half), half)
    mate_rows = pl.ds(pl.multiple_of((1 - d) * half, half), half)

    def f_rows(k):
        at = lax.rem(r - k + nr, nr) * n + d * half
        return pl.ds(pl.multiple_of(at, half), half)

    def bring(i, src, dst):
        load = pltpu.make_async_copy(src, dst, loc_sem.at[i])
        load.start()
        return load

    brought = [
        bring(0, feat_hbm, f_all.at[my_f]),
        bring(1, ws_hbm, ws),
        bring(2, wn_hbm, wn),
        bring(3, cot_hbm.at[own_rows], cot),
    ]

    barrier = pltpu.get_barrier_semaphore()
    peers = [mate]
    peers += [(row_peer(k), c, d) for k in range(1, nr)]
    peers += [(r, col_peer(k), d) for k in range(1, nc)]
    for p in peers:
        pl.semaphore_signal(barrier, inc=1, device_id=p, device_id_type=pl.DeviceIdType.MESH)

    pl.semaphore_wait(barrier, len(peers))
    biasb[...] = jnp.broadcast_to(bias[...], biasb.shape)
    feat_c = {
        k: send(feat_hbm.at[own_rows], f_all.at[f_rows(0)], (row_peer(k), c, d))
        for k in peer_order(nr)
    }
    early = [
        send(ws_hbm, wsx, mate),
        send(wn_hbm, wnx, mate),
        send(cot_hbm.at[mate_rows], cotx, mate),
        send(biasb, biasx, mate),
    ]

    live = counts[0]
    lane = lax.broadcasted_iota(jnp.int32, (slots, slots), 1)
    sub = lax.broadcasted_iota(jnp.int32, (slots, slots), 0)
    pos_row = jnp.broadcast_to(rows_ref[...] * cb + cols_ref[...], (slots, slots))
    pos_row = jnp.where(lane < live, pos_row, rb * cb)
    key_row = pos_row * slots + lane
    key_col = jnp.sum(jnp.where(lane == sub, key_row, 0), axis=1, keepdims=True)
    pos_col = jnp.sum(jnp.where(lane == sub, pos_row, 0), axis=1, keepdims=True)
    rank = jnp.sum((key_row < key_col).astype(jnp.int32), axis=1, keepdims=True)
    hit = rank == lane
    idx_v[0:1, 0:slots] = jnp.sum(jnp.where(hit, sub, 0), axis=0, keepdims=True)
    idx_v[1:2, 0:slots] = jnp.sum(jnp.where(hit, pos_col, 0), axis=0, keepdims=True)
    places = lax.broadcasted_iota(jnp.int32, (slots, rb * cb), 1)
    upto = jnp.sum((pos_col <= places).astype(jnp.int32), axis=0, keepdims=True)
    below = jnp.sum((pos_col < places).astype(jnp.int32), axis=0, keepdims=True)
    idx_v[2:3, 0 : rb * cb] = jnp.where(upto > below, upto - 1, slots)
    to_smem = pltpu.make_async_copy(idx_v, idx_s, loc_sem.at[4])
    to_smem.start()

    run[slots] = jnp.zeros((block, block), BF)
    w_part[...] = jnp.zeros_like(w_part)
    to_smem.wait()
    for load in loads:
        load.wait()

    def merge(k, acc):
        same = idx_s[1, k] == idx_s[1, jnp.maximum(k - 1, 0)]
        acc = jnp.where(same, acc, 0.0) + tiles[idx_s[0, k]].astype(F32)
        run[k] = acc.astype(BF)
        return acc

    acc = jnp.zeros((block, block), F32)
    acc = lax.fori_loop(0, slots // 2, merge, acc, unroll=16)
    pair_c = []
    for k in peer_order(nr):
        feat_c[k].wait_recv()
        pair_c.append(send(f_all.at[f_rows(k)], f_all.at[f_rows(k)], mate))
    lax.fori_loop(slots // 2, slots, merge, acc, unroll=16)

    def merged(first_row, first_col, height, width):
        lines = []
        for i in range(height):
            at = (first_row + i) * cb + first_col
            line = [run[idx_s[2, at + j]] for j in range(width)]
            lines.append(jnp.concatenate(line, axis=1))
        return jnp.concatenate(lines, axis=0)

    for load in brought:
        load.wait()
    for copy in pair_c:
        copy.wait_recv()

    hb = half // block

    def rows_at(owner, part):
        return (owner * 2 + part) * hb

    def product(owner, part):
        return dot(merged(rows_at(owner, part), 0, hb, cb), f_all[...])

    x_c, z_c = {}, {}

    def finish(k):
        x_c[k].wait_recv()
        total = p_own[k] + p_x[k]
        if k == 0:
            p_own[0] = total
        else:
            s_b[k] = total.astype(BF)
            z_c[k] = send(s_b.at[k], z_x.at[k], (r, col_peer(k), d))

    order = peer_order(nc) + [0]
    for i, k in enumerate(order):
        owner = col_peer(k)
        p_mate[k] = product(owner, 1 - d)
        x_c[k] = send(p_mate.at[k], p_x.at[k], mate)
        p_own[k] = product(owner, d)
        if i:
            finish(order[i - 1])
    finish(order[-1])
    for copy in early:
        copy.wait_recv()
    f_own = f_all[f_rows(0), :]
    weights = [(ws[...], wn[...]), (wsx[...], wnx[...])]
    biases = [biasb[0:1, :], biasx[0:1, :]]
    for e in range(2):
        pre_s[e] = dot(f_own, weights[e][0]) + biases[e]
    agg = p_own[0]
    for k in peer_order(nc):
        z_c[k].wait_recv()
        agg = agg + z_x[k].astype(F32)

    hi = agg.astype(BF)
    lo = (agg - hi.astype(F32)).astype(BF)
    cots = [cot[...], cotx[...]]
    grads = []
    u_t = v = None
    for e in range(2):
        w_n = weights[e][1]
        pre = pre_s[e] + dot(hi, w_n) + dot(lo, w_n)
        gate = jax.nn.sigmoid(pre)
        value = (pre * gate).astype(BF)
        if e == 0:
            o_own[...] = value
        else:
            o_mate[...] = value
        g = (cots[e].astype(F32) * gate * (1.0 + pre * (1.0 - gate))).astype(BF)
        grads.append(g)
        term = dot(w_n, g, 1, 1)
        u_t = term if u_t is None else u_t + term
    u_all[0, 0] = u_t.astype(BF)
    u_m = send(u_all.at[0, 0], u_all.at[0, 1], mate)
    u_c = {k: send(u_all.at[0, 0], u_all.at[k, 0], (r, col_peer(k), d)) for k in peer_order(nc)}
    out_c = send(o_mate, out.at[own_rows], mate)
    kept = bring(0, o_own, out.at[own_rows])
    for e in (1, 0):
        g = grads[e]
        w_part[e, 0:f, :] = dot(f_own, g, 0, 0)
        w_part[e, f : 2 * f, :] = dot(hi, g, 0, 0)
        total = jnp.sum(g.astype(F32), axis=0, keepdims=True)
        w_part[e, 2 * f : 2 * f + 8, :] = jnp.broadcast_to(total, (8, hh))
        if e == 1:
            w_c = send(w_part.at[1], w_x, mate)
    v_t[...] = dot(weights[0][0], grads[0], 1, 1) + dot(weights[1][0], grads[1], 1, 1)

    def add_rows(k, e, first):
        owner = lax.rem(c - k + nc, nc)
        at = rows_at(owner, d if e == 0 else 1 - d)
        for q in range(nr):
            for h in range(2):
                term = dot(u_all[k, e], merged(at, (q * 2 + h) * hb, hb, hb))
                g_acc[q, h] = term if first else g_acc[q, h] + term

    add_rows(0, 0, True)

    w_rows = w_x.shape[0]
    wr = w_rows // nr
    wc = wr // nc
    w_c.wait_recv()
    w_part[0] = w_part[0] + w_x[...]
    wr_c = []
    for k in range(1, nr):
        at = pl.ds(pl.multiple_of(row_peer(k) * wr, 8), wr)
        wr_c.append(send(w_part.at[0, at], w_rx.at[k], (row_peer(k), c, d)))

    u_m.wait_recv()
    add_rows(0, 1, False)

    arrivals = list(reversed(peer_order(nc)))
    fwd_c = {}
    for i, k in enumerate(arrivals):
        u_c[k].wait_recv()
        fwd_c[k] = send(u_all.at[k, 0], u_all.at[k, 1], mate)
        if i:
            fwd_c[arrivals[i - 1]].wait_recv()
            add_rows(arrivals[i - 1], 1, False)
        add_rows(k, 0, False)
        if i == 0:
            for copy in wr_c:
                copy.wait_recv()
            total = w_part[0, pl.ds(pl.multiple_of(r * wr, 8), wr), :]
            for k in range(1, nr):
                total = total + w_rx[k]
            w_2[...] = total
            wc_c = []
            for k in range(1, nc):
                at = pl.ds(pl.multiple_of(col_peer(k) * wc, 8), wc)
                wc_c.append(send(w_2.at[at], w_cx.at[k], (r, col_peer(k), d)))

    for copy in wc_c:
        copy.wait_recv()
    total = w_2[pl.ds(pl.multiple_of(c * wc, 8), wc), :]
    for k in range(1, nc):
        total = total + w_cx[k]
    mine = pl.ds(pl.multiple_of(r * wr + c * wc, 8), wc)
    wout[mine, :] = total * (1.0 / jnp.sqrt(jnp.full((1, 1), nr * nc * n, F32)))
    wg_c = [send(wout.at[mine], wout.at[mine], (r, col_peer(k), d)) for k in range(1, nc)]

    last = arrivals[-1]
    fwd_c[last].wait_recv()

    def last_rows(owner, part):
        at = rows_at(lax.rem(c - last + nc, nc), 1 - d)
        blocks = merged(at, (owner * 2 + part) * hb, hb, hb)
        return g_acc[owner, part] + dot(u_all[last, 1], blocks)

    gx_c, gz_c = {}, {}

    def finish_back(k):
        gx_c[k].wait_recv()
        total = g_own[k] + g_x[k]
        if k == 0:
            g_own[0] = total
        else:
            gs_b[k] = total.astype(BF)
            gz_c[k] = send(gs_b.at[k], gz_x.at[k], (row_peer(k), c, d))

    order = peer_order(nr) + [0]
    for i, k in enumerate(order):
        owner = row_peer(k)
        g_mate[k] = last_rows(owner, 1 - d)
        gx_c[k] = send(g_mate.at[k], g_x.at[k], mate)
        g_own[k] = last_rows(owner, d)
        if i:
            finish_back(order[i - 1])
    finish_back(order[-1])

    for copy in wg_c:
        copy.wait_recv()
    whole = pl.ds(pl.multiple_of(r * wr, 8), wr)
    ag_c = [send(wout.at[whole], wout.at[whole], (row_peer(k), c, d)) for k in range(1, nr)]

    total = v_t[...] + g_own[0]
    for k in peer_order(nr):
        gz_c[k].wait_recv()
        total = total + gz_x[k].astype(F32)
    gfeat[...] = total.T.astype(BF)

    kept.wait()
    out_c.wait_recv()
    for copy in ag_c:
        copy.wait_recv()
    for copy in made:
        copy.wait_send()


def hand_out(out, gfeat, wout, out_o, gfeat_o, self_o, neigh_o, bias_o):
    f = self_o.shape[0]
    out_o[...] = out[...]
    gfeat_o[...] = gfeat[...]
    self_o[...] = wout[0:f, :]
    neigh_o[...] = wout[f : 2 * f, :]
    bias_o[...] = wout[2 * f : 2 * f + 1, :]


def body(mesh, features, self_weight, neigh_weight, bias, cotangent, tile_values, tile_rows, tile_cols, tile_counts):
    nr, nc, nd = mesh.shape["row"], mesh.shape["col"], mesh.shape["depth"]
    assert nd == 2
    n, f = features.shape
    hh = self_weight.shape[1]
    slots, block, _ = tile_values.shape
    half = n // nd
    rb, cb = nc * n // block, nr * n // block
    unit = nr * nc * 8
    w_rows = -(-(2 * f + 8) // unit) * unit
    chunks = 8
    width = max(slots, rb * cb)
    copies = 12 + 6 * nr + 6 * nc
    vmem = pl.BlockSpec(memory_space=pltpu.VMEM)
    smem = pl.BlockSpec(memory_space=pltpu.SMEM)
    hbm = pl.BlockSpec(memory_space=pl.ANY)
    dims = (nr, nc, n, block, slots, chunks)
    out, gfeat, wout = pl.pallas_call(
        functools.partial(kernel, dims),
        out_shape=(
            jax.ShapeDtypeStruct((n, hh), BF),
            jax.ShapeDtypeStruct((half, f), BF),
            jax.ShapeDtypeStruct((w_rows, hh), F32),
        ),
        in_specs=[hbm, hbm, hbm, vmem, hbm, vmem, vmem, smem, hbm],
        out_specs=(hbm, vmem, vmem),
        scratch_shapes=[
            pltpu.VMEM((slots, block, block), BF),
            pltpu.VMEM((slots + 1, block, block), BF),
            pltpu.VMEM((nr * n, f), BF),
            pltpu.VMEM((f, hh), BF),
            pltpu.VMEM((f, hh), BF),
            pltpu.VMEM((half, hh), BF),
            pltpu.VMEM((f, hh), BF),
            pltpu.VMEM((f, hh), BF),
            pltpu.VMEM((8, hh), F32),
            pltpu.VMEM((8, hh), F32),
            pltpu.VMEM((half, hh), BF),
            pltpu.VMEM((8, width), jnp.int32),
            pltpu.SMEM((8, width), jnp.int32),
            pltpu.VMEM((nc, half, f), F32),
            pltpu.VMEM((nc, half, f), F32),
            pltpu.VMEM((nc, half, f), F32),
            pltpu.VMEM((nc, half, f), BF),
            pltpu.VMEM((nc, half, f), BF),
            pltpu.VMEM((half, hh), BF),
            pltpu.VMEM((half, hh), BF),
            pltpu.VMEM((nc, 2, f, half), BF),
            pltpu.VMEM((nr, 2, f, half), F32),
            pltpu.VMEM((nr, f, half), F32),
            pltpu.VMEM((nr, f, half), F32),
            pltpu.VMEM((nr, f, half), F32),
            pltpu.VMEM((nr, f, half), BF),
            pltpu.VMEM((nr, f, half), BF),
            pltpu.VMEM((2, w_rows, hh), F32),
            pltpu.VMEM((w_rows, hh), F32),
            pltpu.VMEM((nr, w_rows // nr, hh), F32),
            pltpu.VMEM((w_rows // nr, hh), F32),
            pltpu.VMEM((nc, w_rows // nr // nc, hh), F32),
            pltpu.VMEM((f, half), F32),
            pltpu.VMEM((2, half, hh), F32),
            pltpu.SemaphoreType.DMA((chunks,)),
            pltpu.SemaphoreType.DMA((5,)),
            pltpu.SemaphoreType.DMA((copies,)),
            pltpu.SemaphoreType.DMA((copies,)),
        ],
        compiler_params=pltpu.CompilerParams(
            collective_id=0, has_side_effects=True, vmem_limit_bytes=60 * 1024 * 1024
        ),
        name="sage_layer",
    )(
        features,
        self_weight,
        neigh_weight,
        bias.reshape(1, hh),
        cotangent,
        tile_rows,
        tile_cols,
        tile_counts,
        tile_values,
    )
    out, gfeat, g_self, g_neigh, g_bias = pl.pallas_call(
        hand_out,
        out_shape=(
            jax.ShapeDtypeStruct((n, hh), BF),
            jax.ShapeDtypeStruct((half, f), BF),
            jax.ShapeDtypeStruct((f, hh), F32),
            jax.ShapeDtypeStruct((f, hh), F32),
            jax.ShapeDtypeStruct((1, hh), F32),
        ),
        in_specs=[vmem] * 3,
        out_specs=(vmem,) * 5,
        name="hand_out",
    )(out, gfeat, wout)
    return out, gfeat, g_self, g_neigh, g_bias.reshape(hh)


def solution(mesh):
    placed = (
        P(("row", "col"), None),
        P(None, "depth"),
        P(None, "depth"),
        P("depth"),
        P(("row", "col"), "depth"),
        P(("row", "col", "depth"), None, None),
        P(("row", "col", "depth"), None),
        P(("row", "col", "depth"), None),
        P(("row", "col", "depth")),
    )
    return jax.shard_map(
        functools.partial(body, mesh),
        mesh=mesh,
        in_specs=placed,
        out_specs=(
            P(("row", "col"), "depth"),
            P(("row", "col", "depth"), None),
            P(None, "depth"),
            P(None, "depth"),
            P("depth"),
        ),
        check_vma=False,
    )
```

```python
import functools

import jax
import jax.numpy as jnp
from jax import lax
from jax.experimental import pallas as pl
from jax.experimental.pallas import tpu as pltpu
from jax.sharding import PartitionSpec as P

BF = jnp.bfloat16
F32 = jnp.float32


def dot(a, b, ca=1, cb=0):
    return lax.dot_general(a, b, (((ca,), (cb,)), ((), ())), preferred_element_type=F32)


def peer_order(n):
    return sorted(range(1, n), key=lambda k: (abs(2 * k - n), k))


def kernel(
    dims,
    feat_hbm,
    ws_hbm,
    wn_hbm,
    bias,
    cot_hbm,
    rows_ref,
    cols_ref,
    counts,
    tiles_hbm,
    out,
    gfeat,
    wout,
    tiles,
    run,
    f_all,
    ws,
    wn,
    cot,
    wsx,
    wnx,
    biasb,
    biasx,
    cotx,
    idx_v,
    idx_s,
    p_own,
    p_mate,
    p_x,
    s_b,
    z_x,
    o_own,
    o_mate,
    u_all,
    g_acc,
    g_own,
    g_mate,
    g_x,
    gs_b,
    gz_x,
    w_part,
    w_x,
    w_rx,
    w_2,
    w_cx,
    v_t,
    pre_s,
    tile_sem,
    loc_sem,
    send_sem,
    recv_sem,
):
    nr, nc, n, block, slots, chunks = dims
    f = feat_hbm.shape[1]
    hh = ws.shape[1]
    half = n // 2
    rb = nc * n // block
    cb = nr * n // block
    r, c, d = lax.axis_index("row"), lax.axis_index("col"), lax.axis_index("depth")
    mate = (r, c, 1 - d)

    def row_peer(k):
        return lax.rem(r + k, nr)

    def col_peer(k):
        return lax.rem(c + k, nc)

    made = []

    def send(src, dst, device):
        i = len(made)
        copy = pltpu.make_async_remote_copy(
            src_ref=src,
            dst_ref=dst,
            send_sem=send_sem.at[i],
            recv_sem=recv_sem.at[i],
            device_id=device,
            device_id_type=pl.DeviceIdType.MESH,
        )
        copy.start()
        made.append(copy)
        return copy

    per = slots // chunks
    loads = []
    for i in range(chunks):
        part = pl.ds(i * per, per)
        load = pltpu.make_async_copy(tiles_hbm.at[part], tiles.at[part], tile_sem.at[i])
        load.start()
        loads.append(load)

    my_f = pl.ds(pl.multiple_of(r * n, n), n)
    own_rows = pl.ds(pl.multiple_of(d * half, half), half)
    mate_rows = pl.ds(pl.multiple_of((1 - d) * half, half), half)

    def f_rows(k):
        at = lax.rem(r - k + nr, nr) * n + d * half
        return pl.ds(pl.multiple_of(at, half), half)

    def bring(i, src, dst):
        load = pltpu.make_async_copy(src, dst, loc_sem.at[i])
        load.start()
        return load

    brought = [
        bring(0, feat_hbm, f_all.at[my_f]),
        bring(1, ws_hbm, ws),
        bring(2, wn_hbm, wn),
        bring(3, cot_hbm.at[own_rows], cot),
    ]

    barrier = pltpu.get_barrier_semaphore()
    peers = [mate]
    peers += [(row_peer(k), c, d) for k in range(1, nr)]
    peers += [(r, col_peer(k), d) for k in range(1, nc)]
    for p in peers:
        pl.semaphore_signal(barrier, inc=1, device_id=p, device_id_type=pl.DeviceIdType.MESH)

    live = counts[0]
    lane = lax.broadcasted_iota(jnp.int32, (slots, slots), 1)
    sub = lax.broadcasted_iota(jnp.int32, (slots, slots), 0)
    pos_row = jnp.broadcast_to(rows_ref[...] * cb + cols_ref[...], (slots, slots))
    pos_row = jnp.where(lane < live, pos_row, rb * cb)
    key_row = pos_row * slots + lane
    key_col = jnp.sum(jnp.where(lane == sub, key_row, 0), axis=1, keepdims=True)
    pos_col = jnp.sum(jnp.where(lane == sub, pos_row, 0), axis=1, keepdims=True)
    rank = jnp.sum((key_row < key_col).astype(jnp.int32), axis=1, keepdims=True)
    hit = rank == lane
    idx_v[0:1, 0:slots] = jnp.sum(jnp.where(hit, sub, 0), axis=0, keepdims=True)
    idx_v[1:2, 0:slots] = jnp.sum(jnp.where(hit, pos_col, 0), axis=0, keepdims=True)
    places = lax.broadcasted_iota(jnp.int32, (slots, rb * cb), 1)
    upto = jnp.sum((pos_col <= places).astype(jnp.int32), axis=0, keepdims=True)
    below = jnp.sum((pos_col < places).astype(jnp.int32), axis=0, keepdims=True)
    idx_v[2:3, 0 : rb * cb] = jnp.where(upto > below, upto - 1, slots)
    to_smem = pltpu.make_async_copy(idx_v, idx_s, loc_sem.at[4])
    to_smem.start()

    pl.semaphore_wait(barrier, len(peers))
    biasb[...] = jnp.broadcast_to(bias[...], biasb.shape)
    feat_c = {
        k: send(feat_hbm.at[own_rows], f_all.at[f_rows(0)], (row_peer(k), c, d))
        for k in peer_order(nr)
    }
    early = [
        send(ws_hbm, wsx, mate),
        send(wn_hbm, wnx, mate),
        send(cot_hbm.at[mate_rows], cotx, mate),
        send(biasb, biasx, mate),
    ]
    run[slots] = jnp.zeros((block, block), BF)
    w_part[...] = jnp.zeros_like(w_part)
    to_smem.wait()
    for load in loads:
        load.wait()

    def merge(k, acc):
        same = idx_s[1, k] == idx_s[1, jnp.maximum(k - 1, 0)]
        acc = jnp.where(same, acc, 0.0) + tiles[idx_s[0, k]].astype(F32)
        run[k] = acc.astype(BF)
        return acc

    acc = jnp.zeros((block, block), F32)
    acc = lax.fori_loop(0, slots // 2, merge, acc, unroll=8)
    pair_c = []
    for k in peer_order(nr):
        feat_c[k].wait_recv()
        pair_c.append(send(f_all.at[f_rows(k)], f_all.at[f_rows(k)], mate))
    lax.fori_loop(slots // 2, slots, merge, acc, unroll=8)

    def merged(first_row, first_col, height, width):
        lines = []
        for i in range(height):
            at = (first_row + i) * cb + first_col
            line = [run[idx_s[2, at + j]] for j in range(width)]
            lines.append(jnp.concatenate(line, axis=1))
        return jnp.concatenate(lines, axis=0)

    for load in brought:
        load.wait()
    for copy in pair_c:
        copy.wait_recv()

    hb = half // block

    def rows_at(owner, part):
        return (owner * 2 + part) * hb

    def product(owner, part):
        return dot(merged(rows_at(owner, part), 0, hb, cb), f_all[...])

    x_c, z_c = {}, {}

    def finish(k):
        x_c[k].wait_recv()
        total = p_own[k] + p_x[k]
        if k == 0:
            p_own[0] = total
        else:
            s_b[k] = total.astype(BF)
            z_c[k] = send(s_b.at[k], z_x.at[k], (r, col_peer(k), d))

    order = peer_order(nc) + [0]
    for i, k in enumerate(order):
        owner = col_peer(k)
        p_mate[k] = product(owner, 1 - d)
        x_c[k] = send(p_mate.at[k], p_x.at[k], mate)
        p_own[k] = product(owner, d)
        if i:
            finish(order[i - 1])
    finish(order[-1])
    for copy in early:
        copy.wait_recv()
    f_own = f_all[f_rows(0), :]
    weights = [(ws[...], wn[...]), (wsx[...], wnx[...])]
    biases = [biasb[0:1, :], biasx[0:1, :]]
    for e in range(2):
        pre_s[e] = dot(f_own, weights[e][0]) + biases[e]
    agg = p_own[0]
    for k in peer_order(nc):
        z_c[k].wait_recv()
        agg = agg + z_x[k].astype(F32)

    hi = agg.astype(BF)
    lo = (agg - hi.astype(F32)).astype(BF)
    cots = [cot[...], cotx[...]]
    grads = []
    u_t = v = None
    for e in range(2):
        w_n = weights[e][1]
        pre = pre_s[e] + dot(hi, w_n) + dot(lo, w_n)
        gate = jax.nn.sigmoid(pre)
        value = (pre * gate).astype(BF)
        if e == 0:
            o_own[...] = value
        else:
            o_mate[...] = value
        g = (cots[e].astype(F32) * gate * (1.0 + pre * (1.0 - gate))).astype(BF)
        grads.append(g)
        term = dot(w_n, g, 1, 1)
        u_t = term if u_t is None else u_t + term
    u_all[0, 0] = u_t.astype(BF)
    u_m = send(u_all.at[0, 0], u_all.at[0, 1], mate)
    u_c = {k: send(u_all.at[0, 0], u_all.at[k, 0], (r, col_peer(k), d)) for k in peer_order(nc)}
    out_c = send(o_mate, out.at[own_rows], mate)
    kept = bring(0, o_own, out.at[own_rows])
    for e in (1, 0):
        g = grads[e]
        w_part[e, 0:f, :] = dot(f_own, g, 0, 0)
        w_part[e, f : 2 * f, :] = dot(hi, g, 0, 0)
        total = jnp.sum(g.astype(F32), axis=0, keepdims=True)
        w_part[e, 2 * f : 2 * f + 8, :] = jnp.broadcast_to(total, (8, hh))
        if e == 1:
            w_c = send(w_part.at[1], w_x, mate)
    v_t[...] = dot(weights[0][0], grads[0], 1, 1) + dot(weights[1][0], grads[1], 1, 1)

    def add_rows(k, e, first):
        owner = lax.rem(c - k + nc, nc)
        at = rows_at(owner, d if e == 0 else 1 - d)
        for q in range(nr):
            for h in range(2):
                term = dot(u_all[k, e], merged(at, (q * 2 + h) * hb, hb, hb))
                g_acc[q, h] = term if first else g_acc[q, h] + term

    add_rows(0, 0, True)

    w_rows = w_x.shape[0]
    wr = w_rows // nr
    wc = wr // nc
    w_c.wait_recv()
    w_part[0] = w_part[0] + w_x[...]
    wr_c = []
    for k in range(1, nr):
        at = pl.ds(pl.multiple_of(row_peer(k) * wr, 8), wr)
        wr_c.append(send(w_part.at[0, at], w_rx.at[k], (row_peer(k), c, d)))

    u_m.wait_recv()
    add_rows(0, 1, False)

    for copy in wr_c:
        copy.wait_recv()
    total = w_part[0, pl.ds(pl.multiple_of(r * wr, 8), wr), :]
    for k in range(1, nr):
        total = total + w_rx[k]
    w_2[...] = total
    wc_c = []
    for k in range(1, nc):
        at = pl.ds(pl.multiple_of(col_peer(k) * wc, 8), wc)
        wc_c.append(send(w_2.at[at], w_cx.at[k], (r, col_peer(k), d)))

    arrivals = list(reversed(peer_order(nc)))
    fwd_c = {}
    for i, k in enumerate(arrivals):
        u_c[k].wait_recv()
        fwd_c[k] = send(u_all.at[k, 0], u_all.at[k, 1], mate)
        if i:
            fwd_c[arrivals[i - 1]].wait_recv()
            add_rows(arrivals[i - 1], 1, False)
        add_rows(k, 0, False)

    for copy in wc_c:
        copy.wait_recv()
    total = w_2[pl.ds(pl.multiple_of(c * wc, 8), wc), :]
    for k in range(1, nc):
        total = total + w_cx[k]
    mine = pl.ds(pl.multiple_of(r * wr + c * wc, 8), wc)
    wout[mine, :] = total * (1.0 / jnp.sqrt(jnp.full((1, 1), nr * nc * n, F32)))
    wg_c = [send(wout.at[mine], wout.at[mine], (r, col_peer(k), d)) for k in range(1, nc)]

    last = arrivals[-1]
    fwd_c[last].wait_recv()

    def last_rows(owner, part):
        at = rows_at(lax.rem(c - last + nc, nc), 1 - d)
        blocks = merged(at, (owner * 2 + part) * hb, hb, hb)
        return g_acc[owner, part] + dot(u_all[last, 1], blocks)

    gx_c, gz_c = {}, {}

    def finish_back(k):
        gx_c[k].wait_recv()
        total = g_own[k] + g_x[k]
        if k == 0:
            g_own[0] = total
        else:
            gs_b[k] = total.astype(BF)
            gz_c[k] = send(gs_b.at[k], gz_x.at[k], (row_peer(k), c, d))

    order = peer_order(nr) + [0]
    for i, k in enumerate(order):
        owner = row_peer(k)
        g_mate[k] = last_rows(owner, 1 - d)
        gx_c[k] = send(g_mate.at[k], g_x.at[k], mate)
        g_own[k] = last_rows(owner, d)
        if i:
            finish_back(order[i - 1])
    finish_back(order[-1])

    for copy in wg_c:
        copy.wait_recv()
    whole = pl.ds(pl.multiple_of(r * wr, 8), wr)
    ag_c = [send(wout.at[whole], wout.at[whole], (row_peer(k), c, d)) for k in range(1, nr)]

    total = v_t[...] + g_own[0]
    for k in peer_order(nr):
        gz_c[k].wait_recv()
        total = total + gz_x[k].astype(F32)
    gfeat[...] = total.T.astype(BF)

    kept.wait()
    out_c.wait_recv()
    for copy in ag_c:
        copy.wait_recv()
    for copy in made:
        copy.wait_send()


def hand_out(out, gfeat, wout, out_o, gfeat_o, self_o, neigh_o, bias_o):
    f = self_o.shape[0]
    out_o[...] = out[...]
    gfeat_o[...] = gfeat[...]
    self_o[...] = wout[0:f, :]
    neigh_o[...] = wout[f : 2 * f, :]
    bias_o[...] = wout[2 * f : 2 * f + 1, :]


def body(mesh, features, self_weight, neigh_weight, bias, cotangent, tile_values, tile_rows, tile_cols, tile_counts):
    nr, nc, nd = mesh.shape["row"], mesh.shape["col"], mesh.shape["depth"]
    assert nd == 2
    n, f = features.shape
    hh = self_weight.shape[1]
    slots, block, _ = tile_values.shape
    half = n // nd
    rb, cb = nc * n // block, nr * n // block
    unit = nr * nc * 8
    w_rows = -(-(2 * f + 8) // unit) * unit
    chunks = 8
    width = max(slots, rb * cb)
    copies = 12 + 6 * nr + 6 * nc
    vmem = pl.BlockSpec(memory_space=pltpu.VMEM)
    smem = pl.BlockSpec(memory_space=pltpu.SMEM)
    hbm = pl.BlockSpec(memory_space=pl.ANY)
    dims = (nr, nc, n, block, slots, chunks)
    out, gfeat, wout = pl.pallas_call(
        functools.partial(kernel, dims),
        out_shape=(
            jax.ShapeDtypeStruct((n, hh), BF),
            jax.ShapeDtypeStruct((half, f), BF),
            jax.ShapeDtypeStruct((w_rows, hh), F32),
        ),
        in_specs=[hbm, hbm, hbm, vmem, hbm, vmem, vmem, smem, hbm],
        out_specs=(hbm, vmem, vmem),
        scratch_shapes=[
            pltpu.VMEM((slots, block, block), BF),
            pltpu.VMEM((slots + 1, block, block), BF),
            pltpu.VMEM((nr * n, f), BF),
            pltpu.VMEM((f, hh), BF),
            pltpu.VMEM((f, hh), BF),
            pltpu.VMEM((half, hh), BF),
            pltpu.VMEM((f, hh), BF),
            pltpu.VMEM((f, hh), BF),
            pltpu.VMEM((8, hh), F32),
            pltpu.VMEM((8, hh), F32),
            pltpu.VMEM((half, hh), BF),
            pltpu.VMEM((8, width), jnp.int32),
            pltpu.SMEM((8, width), jnp.int32),
            pltpu.VMEM((nc, half, f), F32),
            pltpu.VMEM((nc, half, f), F32),
            pltpu.VMEM((nc, half, f), F32),
            pltpu.VMEM((nc, half, f), BF),
            pltpu.VMEM((nc, half, f), BF),
            pltpu.VMEM((half, hh), BF),
            pltpu.VMEM((half, hh), BF),
            pltpu.VMEM((nc, 2, f, half), BF),
            pltpu.VMEM((nr, 2, f, half), F32),
            pltpu.VMEM((nr, f, half), F32),
            pltpu.VMEM((nr, f, half), F32),
            pltpu.VMEM((nr, f, half), F32),
            pltpu.VMEM((nr, f, half), BF),
            pltpu.VMEM((nr, f, half), BF),
            pltpu.VMEM((2, w_rows, hh), F32),
            pltpu.VMEM((w_rows, hh), F32),
            pltpu.VMEM((nr, w_rows // nr, hh), F32),
            pltpu.VMEM((w_rows // nr, hh), F32),
            pltpu.VMEM((nc, w_rows // nr // nc, hh), F32),
            pltpu.VMEM((f, half), F32),
            pltpu.VMEM((2, half, hh), F32),
            pltpu.SemaphoreType.DMA((chunks,)),
            pltpu.SemaphoreType.DMA((5,)),
            pltpu.SemaphoreType.DMA((copies,)),
            pltpu.SemaphoreType.DMA((copies,)),
        ],
        compiler_params=pltpu.CompilerParams(
            collective_id=0, has_side_effects=True, vmem_limit_bytes=60 * 1024 * 1024
        ),
        name="sage_layer",
    )(
        features,
        self_weight,
        neigh_weight,
        bias.reshape(1, hh),
        cotangent,
        tile_rows,
        tile_cols,
        tile_counts,
        tile_values,
    )
    out, gfeat, g_self, g_neigh, g_bias = pl.pallas_call(
        hand_out,
        out_shape=(
            jax.ShapeDtypeStruct((n, hh), BF),
            jax.ShapeDtypeStruct((half, f), BF),
            jax.ShapeDtypeStruct((f, hh), F32),
            jax.ShapeDtypeStruct((f, hh), F32),
            jax.ShapeDtypeStruct((1, hh), F32),
        ),
        in_specs=[vmem] * 3,
        out_specs=(vmem,) * 5,
        name="hand_out",
    )(out, gfeat, wout)
    return out, gfeat, g_self, g_neigh, g_bias.reshape(hh)


def solution(mesh):
    placed = (
        P(("row", "col"), None),
        P(None, "depth"),
        P(None, "depth"),
        P("depth"),
        P(("row", "col"), "depth"),
        P(("row", "col", "depth"), None, None),
        P(("row", "col", "depth"), None),
        P(("row", "col", "depth"), None),
        P(("row", "col", "depth")),
    )
    return jax.shard_map(
        functools.partial(body, mesh),
        mesh=mesh,
        in_specs=placed,
        out_specs=(
            P(("row", "col"), "depth"),
            P(("row", "col", "depth"), None),
            P(None, "depth"),
            P(None, "depth"),
            P("depth"),
        ),
        check_vma=False,
    )
```
